32 devices in a mesh: geo: 4 (over x, core), spec: 8 (over z, y).
Axes of the slice: x: 2, y: 2, z: 4, core: 2. Of those that a mesh axis runs over, the one named last changes fastest.
Arguments:
- spectrum: float32 [32, 36, 128, 512], P('spec', None, 'geo'), may hold values from 0.01 to 50, as said below
- land_sea: int32 [128, 512], P('geo'), may hold values from 0 to 1, as said below
- sea_index: int32 [4, 12288], P('geo'), may hold values from 0 to 16383, as said below
- sea_count: int32 [4], P('geo'), may hold values from 4096 to 12288, as said below
- wind_speed: float32 [128, 512], P('geo'), may hold values from 4 to 24
- wind_dir: float32 [128, 512], P('geo'), may hold values from -3.140625 to 3.140625
- slope_x: float32 [128, 512], P('geo'), may hold values from -0.5 to 0.5
- slope_y: float32 [128, 512], P('geo'), may hold values from -0.5 to 0.5
Outputs:
- next_spectrum: float32 [32, 36, 128, 512], P('spec', None, 'geo')
The draws below stay inside these ranges and needn't reach their ends.
Inputs may be any that keep to these rules, and one draw needn't show every extreme that they name: `spectrum`: A positive energy density. `land_sea`: land comes in aligned 8 x 8 blocks of cells. `sea_index`: row t lists the sea cells of tile t in increasing position, then its land cells in increasing position, all distinct; its first sea_count[t] entries are exactly the tile's sea cells. `sea_count`: the number of sea cells of each tile; at least one tile has exactly 12288.
All inputs are finite; a program needn't handle non-finite values.
Results may differ from the reference program's by a relative error of at most 0.0003.
Values sent between devices are 32-bit elements; how exact they have to be, the bound alone decides.
No kernel may reach another device: no remote copies, remote signals or barrier semaphores. Data moves between devices by JAX's collectives and lax.ppermute only.
A program may use at most 128 MiB of HBM per device.

```python
import math
import jax
import jax.numpy as jnp
from jax import lax

NK = 32
NTH = 36
ROWS = 32
NY = 512
TILES = 4
NX = 128
CAP = 12288


def log_uniform(key, shape, low, high):
    return jnp.exp(jax.random.uniform(key, shape, jnp.float32, jnp.log(low), jnp.log(high)))


def draw_spectrum(key, part):
    base = jax.random.fold_in(key, 11)
    key_freq, key_dirs, key_rough = jax.random.split(base, 3)
    freq_scale = log_uniform(key_freq, (NK, 1, 1, 1), 0.3, 3.0)
    dir_scale = log_uniform(key_dirs, (1, NTH, 1, 1), 0.5, 2.0)
    rough = log_uniform(key_rough, (NK, NTH, NX, NY), 0.5, 2.0)
    return freq_scale * dir_scale * rough


def land_layout(key):
    base = jax.random.fold_in(key, 7)
    key_lands, key_full, key_order = jax.random.split(base, 3)
    block_rows = ROWS // 8
    block_cols = NY // 8
    block_count = block_rows * block_cols
    fewest = block_count // 4
    most_land = 3 * block_count // 4
    land_counts = jax.random.randint(key_lands, (TILES,), fewest, most_land + 1)
    full_tile = jax.random.randint(key_full, (), 0, TILES)
    land_counts = jnp.where(jnp.arange(TILES) == full_tile, fewest, land_counts)
    orders = jax.vmap(lambda one_key: jax.random.permutation(one_key, block_count))(jax.random.split(key_order, TILES))
    block_ranks = jnp.argsort(orders, axis=1, stable=True)
    land_blocks = (block_ranks < land_counts[:, None]).astype(jnp.int32).reshape(TILES, block_rows, block_cols)
    sea_tiles = 1 - jnp.repeat(jnp.repeat(land_blocks, 8, axis=1), 8, axis=2)
    flat_sea = sea_tiles.reshape(TILES, ROWS * NY)
    order_keys = (1 - flat_sea) * (ROWS * NY) + jnp.arange(ROWS * NY, dtype=jnp.int32)[None, :]
    listing = jnp.argsort(order_keys, axis=1, stable=True)[:, :CAP].astype(jnp.int32)
    counts = jnp.sum(flat_sea, axis=1).astype(jnp.int32)
    return (sea_tiles.reshape(TILES * ROWS, NY).astype(jnp.int32), listing, counts)


def draw_land_sea(key, part):
    return land_layout(key)[0]


def draw_sea_index(key, part):
    return land_layout(key)[1]


def draw_sea_count(key, part):
    return land_layout(key)[2]


def block_scale(rng, extent, cuts, low, largest):
    loudness, own = 1.0, jax.random.fold_in(rng, 6)
    for position, blocks in cuts:
        heights = jnp.exp(jax.random.uniform(jax.random.fold_in(own, position), (blocks,), jnp.float32, low / len(cuts), largest / len(cuts)))
        loudness = loudness * jnp.repeat(heights, extent[position] // blocks).reshape([-1 if axis == position else 1 for axis in range(len(extent))])
    return loudness


def setup_inputs(seed: int = 0) -> dict:
    seeds = jax.random.split(jax.random.key(seed), 9)
    spectrum = draw_spectrum(jax.random.fold_in(seeds[8], 71), 0)
    land_sea = draw_land_sea(jax.random.fold_in(seeds[8], 71), 0)
    sea_index = draw_sea_index(jax.random.fold_in(seeds[8], 71), 0)
    sea_count = draw_sea_count(jax.random.fold_in(seeds[8], 71), 0)
    wind_speed = jnp.clip(4.0 + 20.0 * jax.random.uniform(seeds[4], (NX, NY), jnp.float32) ** block_scale(seeds[4], (NX, NY), ((0, 4),), -0.2, 0.2), 4.0, 24.0)
    wind_dir = jnp.clip(jax.random.uniform(seeds[5], (NX, NY), jnp.float32, -3.140625, 3.140625), -3.140625, 3.140625)
    slope_x = jnp.clip(jax.random.uniform(seeds[6], (NX, NY), jnp.float32, -0.5, 0.5) * block_scale(seeds[6], (NX, NY), ((0, 4),), -0.4, 0.0), -0.5, 0.5)
    slope_y = jnp.clip(jax.random.uniform(seeds[7], (NX, NY), jnp.float32, -0.5, 0.5) * block_scale(seeds[7], (NX, NY), ((0, 4),), -0.4, 0.0), -0.5, 0.5)
    return {"spectrum": spectrum, "land_sea": land_sea, "sea_index": sea_index, "sea_count": sea_count, "wind_speed": wind_speed, "wind_dir": wind_dir, "slope_x": slope_x, "slope_y": slope_y}


GRAVITY = 9.81
BASE_FREQ = 0.035
GROWTH = 1.1
COURANT_TOP = 0.9
TURN_TOP = 1.2
SPACING = 0.1
USTAR_RATIO = 0.035
WIND_COEF = 0.0375
WHITECAP = 0.36
STEEP_REF = 1.6
EPSILON = 1e-06
QUAD_COEF = 100.0

def band_table(band_ids):
    growth_factor = jnp.power(GROWTH, band_ids)
    radian_freq = 2.0 * math.pi * BASE_FREQ * growth_factor
    wavenum = radian_freq * radian_freq / GRAVITY
    return (radian_freq, wavenum, COURANT_TOP / growth_factor, TURN_TOP / growth_factor, SPACING * radian_freq)

def quick_flux(far_left, near_left, near_right, far_right, courant):
    forward = courant >= 0
    upwind = jnp.where(forward, far_left, far_right)
    center = jnp.where(forward, near_left, near_right)
    downwind = jnp.where(forward, near_right, near_left)
    face_value = 0.5 * (center + downwind) - 0.5 * jnp.abs(courant) * (downwind - center) - (1.0 - courant * courant) / 6.0 * (downwind - 2.0 * center + upwind)
    return courant * face_value

def advect(padded, courant, along):
    face_count = padded.shape[along] - 4
    shifted = [lax.slice_in_dim(padded, offset, offset + face_count + 1, axis=along) for offset in range(4)]
    face_flux = quick_flux(shifted[0], shifted[1], shifted[2], shifted[3], courant)
    centre_cells = lax.slice_in_dim(padded, 2, 2 + face_count, axis=along)
    upper_flux = lax.slice_in_dim(face_flux, 1, face_count + 1, axis=along)
    lower_flux = lax.slice_in_dim(face_flux, 0, face_count, axis=along)
    return centre_cells - (upper_flux - lower_flux)

def quad_delta(center, above, below, energy, dir_axis):
    plus = jnp.roll(above, -1, axis=dir_axis)
    minus = jnp.roll(below, 3, axis=dir_axis)
    return QUAD_COEF * (center * center * (plus + minus) - 2.0 * center * plus * minus) / (energy * energy)

def quad_term(delta, delta_above, delta_below, dir_axis):
    return -2.0 * delta + jnp.roll(delta_below, 1, axis=dir_axis) + jnp.roll(delta_above, -3, axis=dir_axis)

def sources(density, energy_sum, first_sum, root_sum, radian_freq, wavenum, cosine, wind_speed):
    energy = energy_sum + EPSILON
    mean_sigma = energy / (first_sum + EPSILON)
    ratio_k = energy / (root_sum + EPSILON)
    mean_k = ratio_k * ratio_k
    steepness = energy * mean_k * mean_k / STEEP_REF
    decay_rate = WHITECAP * mean_sigma * (wavenum / mean_k) * steepness * steepness
    growth_rate = WIND_COEF * radian_freq * jnp.maximum(28.0 * USTAR_RATIO * wind_speed * radian_freq / GRAVITY * cosine - 1.0, 0.0)
    return density * (1.0 + growth_rate) / (1.0 + decay_rate)

def reference(spectrum, land_sea, sea_index, sea_count, wind_speed, wind_dir, slope_x, slope_y):
    wet_mask = land_sea.astype(jnp.float32)
    dtheta = 2.0 * math.pi / NTH
    angles = (jnp.arange(NTH).astype(jnp.float32) + 0.5) * dtheta
    face_angles = jnp.arange(NTH + 1).astype(jnp.float32) * dtheta
    cosine = jnp.cos(angles[:, None, None] - wind_dir[None])

    def propagate(member):
        density, band = member
        radian_freq, wavenum, courant, turn_rate, band_spread = band_table(band)
        density = density * wet_mask
        padded = jnp.pad(density, ((0, 0), (2, 2), (0, 0)))
        density = advect(padded, courant * jnp.cos(angles)[:, None, None], 1) * wet_mask
        padded = jnp.pad(density, ((0, 0), (0, 0), (2, 2)))
        density = advect(padded, courant * jnp.sin(angles)[:, None, None], 2) * wet_mask
        turning = turn_rate * (jnp.sin(face_angles)[:, None, None] * slope_x - jnp.cos(face_angles)[:, None, None] * slope_y)
        padded = jnp.concatenate([density[-2:], density, density[:2]], axis=0)
        floored = jnp.maximum(advect(padded, turning, 0), 0.0)
        scaled = floored * (band_spread * dtheta)
        return (floored, lax.optimization_barrier(jnp.sum(scaled, axis=0)), lax.optimization_barrier(jnp.sum(scaled / radian_freq, axis=0)), lax.optimization_barrier(jnp.sum(scaled / jnp.sqrt(wavenum), axis=0)))
    band_ids = jnp.arange(NK).astype(jnp.float32)
    band_slots = jnp.arange(NK).astype(jnp.int32)
    floored, energy_part, first_part, root_part = lax.map(propagate, (spectrum, band_ids))
    energy_sum = lax.optimization_barrier(jnp.sum(energy_part, axis=0))
    first_sum = lax.optimization_barrier(jnp.sum(first_part, axis=0))
    root_sum = lax.optimization_barrier(jnp.sum(root_part, axis=0))
    energy = energy_sum + EPSILON
    zero_band = jnp.zeros((1,) + floored.shape[1:], jnp.float32)
    padded_bands = jnp.concatenate([zero_band, floored, zero_band], axis=0)

    def pairing(index):
        return quad_delta(padded_bands[index + 1], padded_bands[index + 2], padded_bands[index], energy, 0)
    delta = lax.map(pairing, band_slots)
    padded_delta = jnp.concatenate([zero_band, delta, zero_band], axis=0)

    def update(member):
        density, band, index = member
        radian_freq, wavenum, courant, turn_rate, band_spread = band_table(band)
        extra = quad_term(padded_delta[index + 1], padded_delta[index + 2], padded_delta[index], 0)
        return sources(density, energy_sum, first_sum, root_sum, radian_freq, wavenum, cosine, wind_speed) + extra
    updated = lax.map(update, (floored, band_ids, band_slots))
    tile_ids = jnp.arange(TILES).astype(jnp.int32)[:, None]
    global_cells = (tile_ids * (ROWS * NY) + sea_index.astype(jnp.int32)).reshape(-1)
    live_slots = (jnp.arange(CAP).astype(jnp.int32)[None, :] < sea_count[:, None]).astype(jnp.float32).reshape(-1)
    active = jnp.zeros((NX * NY,), jnp.float32).at[global_cells].max(live_slots).reshape(NX, NY)
    return updated * active[None, None]
```

```python
import functools
import math

import jax
import jax.numpy as jnp
import numpy as np
from jax import lax
from jax.experimental import pallas as pl
from jax.experimental.pallas import tpu as pltpu
from jax.sharding import PartitionSpec as P

GRAVITY = 9.81
BASE_FREQ = 0.035
GROWTH = 1.1
COURANT_TOP = 0.9
TURN_TOP = 1.2
SPACING = 0.1
USTAR_RATIO = 0.035
WIND_COEF = 0.0375
WHITECAP = 0.36
STEEP_REF = 1.6
EPSILON = 1e-06
QUAD_COEF = 100.0

STRIP = 8
LANES = 128
VMEM_BYTES = 56 * 1024 * 1024


def tables(band_total, dir_count):
    dtheta = 2.0 * math.pi / dir_count
    angles = (np.arange(dir_count) + 0.5) * dtheta
    faces = np.arange(dir_count) * dtheta
    parts = [
        np.abs(np.cos(angles)),
        np.abs(np.sin(angles)),
        np.sin(faces),
        np.cos(faces),
        np.cos(angles),
        np.sin(angles),
        GROWTH ** np.arange(band_total),
    ]
    return np.concatenate(parts).astype(np.float32)


def sign_runs(dir_count):
    angles = (np.arange(dir_count) + 0.5) * 2.0 * math.pi / dir_count
    signs = [(bool(np.cos(a) >= 0), bool(np.sin(a) >= 0)) for a in angles]
    runs, first = [], 0
    for j in range(1, dir_count + 1):
        if j == dir_count or signs[j] != signs[first]:
            runs.append((first, j) + signs[first])
            first = j
    return runs


def plan_kernel(kept, spill, land_ref, *out_refs):
    cols = land_ref.shape[1]
    flags = [land_ref[STRIP * s : STRIP * s + 1, :].astype(jnp.float32) for s in (spill,) + tuple(kept)]
    rows = [flags[0]] + [1.0 - flag for flag in flags[1:]]
    rows += [jnp.zeros((1, cols), jnp.float32)] * (8 - len(rows))
    table = jnp.concatenate(rows, axis=0)
    first = lax.broadcasted_iota(jnp.int32, (cols, cols), 0)
    second = lax.broadcasted_iota(jnp.int32, (cols, cols), 1)
    block = STRIP
    before = jnp.where(
        jnp.logical_and(first < second // block * block, first % block == 0), 1.0, 0.0
    ).astype(jnp.bfloat16)
    before_t = jnp.where(
        jnp.logical_and(second < first // block * block, second % block == 0), 1.0, 0.0
    ).astype(jnp.bfloat16)
    same = jnp.where(first == second, 1.0, 0.0).astype(jnp.bfloat16)
    narrow = table.astype(jnp.bfloat16)
    ranks = jnp.dot(narrow, before, preferred_element_type=jnp.float32)
    dims = (((1,), (1,)), ((), ()))
    rank_col = lax.dot_general(before_t, narrow, dims, preferred_element_type=jnp.float32)[:, 0:1]
    flag_col = lax.dot_general(same, narrow, dims, preferred_element_type=jnp.float32)[:, 0:1]
    wanted = jnp.where(flag_col > 0.5, rank_col, -1.0)
    phase = first % block == second % block
    offset = jnp.zeros((1, 1), jnp.float32)
    for index, out_ref in enumerate(out_refs):
        hole = table[index + 1 : index + 2, :]
        place = jnp.where(hole > 0.5, ranks[index + 1 : index + 2, :] + offset, -2.0)
        match = jnp.logical_and(phase, jnp.abs(wanted - place) < 0.5)
        out_ref[...] = jnp.where(match, 1.0, 0.0).astype(jnp.bfloat16)
        offset = offset + jnp.sum(hole, axis=1, keepdims=True) * (1.0 / block)


def plan(land_sea, kept, spill):
    cols = land_sea.shape[1]
    return pl.pallas_call(
        functools.partial(plan_kernel, kept, spill),
        out_shape=[jax.ShapeDtypeStruct((cols, cols), jnp.bfloat16)] * len(kept),
        compiler_params=pltpu.CompilerParams(vmem_limit_bytes=VMEM_BYTES),
        name="plan",
    )(land_sea)


def taps(courant):
    rest = (1.0 - courant * courant) * (1.0 / 6.0)
    down = courant * (0.5 - 0.5 * courant - rest)
    centre = courant * (0.5 + 0.5 * courant + 2.0 * rest)
    far = -courant * rest
    return -down, 1.0 - centre + down, centre - far, far


def row_shift(before, cells, after, shift, row_ids):
    if shift > 0:
        return jnp.where(row_ids < shift, pltpu.roll(before, shift, 0), pltpu.roll(cells, shift, 0))
    count = cells.shape[0]
    return jnp.where(
        row_ids >= count + shift, pltpu.roll(after, count + shift, 0), pltpu.roll(cells, count + shift, 0)
    )


def lane_shift(pieces, shift, lane_ids):
    rolled = [pltpu.roll(piece, shift % LANES, 1) for piece in pieces]
    zero = jnp.zeros_like(pieces[0])
    moved = []
    for index in range(len(pieces)):
        if shift > 0:
            other = rolled[index - 1] if index > 0 else zero
            moved.append(jnp.where(lane_ids < shift, other, rolled[index]))
        else:
            other = rolled[index + 1] if index + 1 < len(pieces) else zero
            moved.append(jnp.where(lane_ids >= LANES + shift, other, rolled[index]))
    return moved


def exact_dot(cells, chooser, split_ref, dims):
    count = cells.shape[0]
    high = cells.astype(jnp.bfloat16)
    rest = cells - high.astype(jnp.float32)
    mid = rest.astype(jnp.bfloat16)
    low = (rest - mid.astype(jnp.float32)).astype(jnp.bfloat16)
    split_ref[0:count, :] = high
    split_ref[count : 2 * count, :] = mid
    split_ref[2 * count : 3 * count, :] = low
    product = lax.dot_general(split_ref[...], chooser, dims, preferred_element_type=jnp.float32)
    return product[0:count] + product[count : 2 * count] + product[2 * count : 3 * count]


def propagate_kernel(strips, spill_slot, dests, edge, group, band_total, dir_count, local_bands, *refs):
    refs = list(refs)
    pos_ref, tab_ref, spec_ref, land_ref, sx_ref, sy_ref = refs[:6]
    refs = refs[6:]
    lower_ref = upper_ref = spill_ref = None
    if edge:
        lower_ref, upper_ref, spill_ref = refs[:3]
        refs = refs[3:]
    choosers = refs[: len(dests)]
    refs = refs[len(dests) :]
    out_refs = refs[: len(strips)]
    refs = refs[len(strips) :]
    send_refs = refs[: len(dests)]
    refs = refs[len(dests) :]
    sum_ref = refs[0]
    refs = refs[1:]
    head_ref = tail_ref = None
    if not edge:
        head_ref, tail_ref = refs[:2]
        refs = refs[2:]
    turn_ref, moved_ref, split_ref = refs

    row_count, cols = land_ref.shape
    step = pl.program_id(0)
    band = pos_ref[0] * local_bands + group + step
    growth = tab_ref[6 * dir_count + band]
    courant = COURANT_TOP / growth
    turn_rate = TURN_TOP / growth
    radian_freq = (2.0 * math.pi * BASE_FREQ) * growth
    weight = SPACING * radian_freq * (2.0 * math.pi / dir_count)
    row_ids = lax.broadcasted_iota(jnp.int32, (STRIP, cols), 0)
    lane_ids = lax.broadcasted_iota(jnp.int32, (STRIP, LANES), 1)

    def wet(s):
        return land_ref[STRIP * s : STRIP * (s + 1), :].astype(jnp.float32)

    @pl.when(step == 0)
    def _():
        sum_ref[...] = jnp.zeros_like(sum_ref)

        @pl.loop(0, dir_count)
        def _(f):
            face_sin = tab_ref[2 * dir_count + f]
            face_cos = tab_ref[3 * dir_count + f]
            for slot, s in enumerate(strips):
                rows = slice(STRIP * s, STRIP * (s + 1))
                turn_ref[slot, f] = face_sin * sx_ref[rows, :] - face_cos * sy_ref[rows, :]

    if not edge:
        wet_head = land_ref[0:2, :].astype(jnp.float32)
        wet_tail = land_ref[row_count - 2 : row_count, :].astype(jnp.float32)

    for first, last, cos_up, sin_up in sign_runs(dir_count):

        @pl.loop(first, last)
        def _(j):
            row_taps = taps(courant * tab_ref[j])
            col_taps = taps(courant * tab_ref[dir_count + j])
            if not edge:
                head_ref[0, j] = spec_ref[0, j, 0:2, :] * wet_head
                tail_ref[0, j] = spec_ref[0, j, row_count - 2 : row_count, :] * wet_tail
            for slot, s in enumerate(strips):
                wet_s = wet(s)
                cells = spec_ref[0, j, STRIP * s : STRIP * (s + 1), :] * wet_s
                if s == 0:
                    before = jnp.concatenate(
                        [jnp.zeros((STRIP - 2, cols), jnp.float32), lower_ref[0, j]], axis=0
                    )
                else:
                    before = spec_ref[0, j, STRIP * (s - 1) : STRIP * s, :] * wet(s - 1)
                if STRIP * (s + 1) == row_count:
                    after = jnp.concatenate(
                        [upper_ref[0, j], jnp.zeros((STRIP - 2, cols), jnp.float32)], axis=0
                    )
                else:
                    after = spec_ref[0, j, STRIP * (s + 1) : STRIP * (s + 2), :] * wet(s + 1)
                way = 1 if cos_up else -1
                cells = (
                    row_taps[1] * cells
                    + row_taps[0] * row_shift(before, cells, after, -way, row_ids)
                    + row_taps[2] * row_shift(before, cells, after, way, row_ids)
                    + row_taps[3] * row_shift(before, cells, after, 2 * way, row_ids)
                ) * wet_s
                way = 1 if sin_up else -1
                pieces = [cells[:, LANES * c : LANES * (c + 1)] for c in range(cols // LANES)]
                down = lane_shift(pieces, -way, lane_ids)
                upwind = lane_shift(pieces, way, lane_ids)
                far = lane_shift(pieces, 2 * way, lane_ids)
                for c in range(cols // LANES):
                    lanes = slice(LANES * c, LANES * (c + 1))
                    moved_ref[slot, j + 2, :, lanes] = (
                        col_taps[1] * pieces[c]
                        + col_taps[0] * down[c]
                        + col_taps[2] * upwind[c]
                        + col_taps[3] * far[c]
                    ) * wet_s[:, lanes]

    for slot, s in enumerate(strips):
        moved_ref[slot, 0:2] = moved_ref[slot, dir_count : dir_count + 2]
        moved_ref[slot, dir_count + 2 : dir_count + 4] = moved_ref[slot, 2:4]

        def face_flux(f, turning):
            far_left, left = moved_ref[slot, f], moved_ref[slot, f + 1]
            right, far_right = moved_ref[slot, f + 2], moved_ref[slot, f + 3]
            rate = turn_rate * turning
            square = rate * rate
            slope = right - left
            bend = jnp.where(rate >= 0, slope - (left - far_left), (far_right - right) - slope)
            return rate * (
                0.5 * ((left + right) - rate * slope) - (1.0 / 6.0 - square * (1.0 / 6.0)) * bend
            )

        def turn(f, carry):
            lower, total = carry
            flux = face_flux(f, turn_ref[slot, lax.rem(f, dir_count)])
            cell = jnp.maximum(moved_ref[slot, f + 1] - (flux - lower), 0.0)
            out_refs[slot][0, f - 1] = cell
            return flux, total + cell

        flux = face_flux(0, turn_ref[slot, 0])
        _, total = lax.fori_loop(1, dir_count + 1, turn, (flux, jnp.zeros((STRIP, cols), jnp.float32)))
        rows = slice(STRIP * slot, STRIP * (slot + 1))
        sum_ref[0, rows, :] += weight * total
        sum_ref[1, rows, :] += (SPACING * 2.0 * math.pi / dir_count) * total

    source = spill_ref if edge else out_refs[spill_slot]
    spill = source[0].reshape(dir_count * STRIP, cols)
    for chooser, dest, send_ref in zip(choosers, dests, send_refs):
        filled = exact_dot(spill, chooser[...], split_ref, (((1,), (0,)), ((), ())))
        send_ref[0] = out_refs[dest][0] + filled.reshape(dir_count, STRIP, cols)


def propagate(strips, spill_slot, dests, edge, group, size, band_total, pos, table, spectrum, land_sea, slope_x, slope_y, extra, choosers):
    local_bands, dir_count, row_count, cols = spectrum.shape
    whole = lambda shape: pl.BlockSpec(shape, lambda b: (0,) * len(shape))
    one = lambda rows: pl.BlockSpec((1, dir_count, rows, cols), lambda b: (b, 0, 0, 0))
    smem = pl.BlockSpec(memory_space=pltpu.SMEM)
    flat = whole((row_count, cols))
    in_specs = [smem, smem]
    in_specs += [pl.BlockSpec((1, dir_count, row_count, cols), lambda b: (b + group, 0, 0, 0))]
    in_specs += [flat, flat, flat]
    if edge:
        halo = pl.BlockSpec((1, dir_count, 2, cols), lambda b: (b, 0, 0, 0))
        in_specs += [halo, halo, one(STRIP)]
    in_specs += [whole((cols, cols))] * len(choosers)
    band_array = lambda rows: jax.ShapeDtypeStruct((size, dir_count, rows, cols), jnp.float32)
    out_shape = [band_array(STRIP)] * (len(strips) + len(dests))
    out_specs = [one(STRIP)] * (len(strips) + len(dests))
    sums = (2, STRIP * len(strips), cols)
    out_shape.append(jax.ShapeDtypeStruct(sums, jnp.float32))
    out_specs.append(whole(sums))
    if not edge:
        out_shape += [band_array(2)] * 2
        out_specs += [one(2)] * 2
    cells = size * dir_count * len(strips) * STRIP * cols
    return pl.pallas_call(
        functools.partial(
            propagate_kernel, strips, spill_slot, dests, edge, group, band_total, dir_count, local_bands
        ),
        grid=(size,),
        in_specs=in_specs,
        out_specs=out_specs,
        out_shape=out_shape,
        scratch_shapes=[
            pltpu.VMEM((len(strips), dir_count, STRIP, cols), jnp.float32),
            pltpu.VMEM((len(strips), dir_count + 4, STRIP, cols), jnp.float32),
            pltpu.VMEM((3 * dir_count * STRIP, cols), jnp.bfloat16),
        ],
        compiler_params=pltpu.CompilerParams(vmem_limit_bytes=VMEM_BYTES),
        cost_estimate=pl.CostEstimate(flops=60 * cells, bytes_accessed=16 * cells, transcendentals=0),
        name="propagate_edge" if edge else "propagate_inner",
    )(pos, table, spectrum, land_sea, slope_x, slope_y, *extra, *choosers)


def source_kernel(strip, band_total, dir_count, local_bands, group_count, below_shape, above_shape, spill_count, first_call, *refs):
    refs = list(refs)
    pos_ref, tab_ref, land_ref, wind_ref, sum_ref = refs[:5]
    refs = refs[5:]
    own = refs[:group_count]
    refs = refs[group_count:]
    below = refs[: below_shape * max(spill_count, 1)]
    refs = refs[below_shape * max(spill_count, 1) :]
    above = refs[: above_shape * max(spill_count, 1)]
    refs = refs[above_shape * max(spill_count, 1) :]
    choosers = refs[:spill_count]
    refs = refs[spill_count:]
    if not first_call:
        refs = refs[1:]
    out_ref = refs[0]
    delta_ref = refs[1]
    lanes = out_ref.shape[-1]
    if spill_count:
        split_ref, halo_ref = refs[2:4]
        per_side = below[0].shape[0]
        lists = []
        slot = 0
        for side, count in ((below, below_shape), (above, above_shape)):
            found = []
            for part in range(count):
                for member in range(per_side):
                    total = None
                    for d in range(spill_count):
                        cells = side[d * count + part][member]
                        piece = exact_dot(
                            cells.reshape(dir_count * STRIP, cells.shape[-1]),
                            choosers[d][...],
                            split_ref,
                            (((1,), (1,)), ((), ())),
                        )
                        total = piece if total is None else total + piece
                    halo_ref[slot] = total.reshape(dir_count, STRIP, lanes)
                    found.append((halo_ref, slot))
                    slot += 1
            lists.append(found)
        below_list, above_list = lists
    else:
        below_list = [(ref, i) for ref in below for i in range(ref.shape[0])]
        above_list = [(ref, i) for ref in above for i in range(ref.shape[0])]
    own_list = [(ref, i) for ref in own for i in range(ref.shape[0])]
    bands = below_list + own_list + above_list

    def density(index, j):
        ref, slot = bands[index + 2]
        return ref[slot, j]

    energy = sum_ref[0] + EPSILON
    first_sum = sum_ref[1]
    mean_sigma = energy / (first_sum + EPSILON)
    ratio = energy / (math.sqrt(GRAVITY) * first_sum + EPSILON)
    mean_k = ratio * ratio
    steepness = energy * mean_k * mean_k / STEEP_REF
    decay = WHITECAP * mean_sigma / mean_k * steepness * steepness
    active = land_ref[...].astype(jnp.float32)
    quad_scale = active * QUAD_COEF / (energy * energy)

    @pl.loop(0, dir_count)
    def _(j):
        up = lax.rem(j + 1, dir_count)
        back = lax.rem(j + dir_count - 3, dir_count)
        for index in range(-1, local_bands + 1):
            center = density(index, j)
            plus = density(index + 1, up)
            minus = density(index - 1, back)
            delta_ref[index + 1, j] = center * (center * (plus + minus) - 2.0 * (plus * minus))

    growths, keeps = [], []
    for index in range(local_bands):
        growth = tab_ref[6 * dir_count + pos_ref[0] * local_bands + index]
        radian_freq = (2.0 * math.pi * BASE_FREQ) * growth
        wavenum = radian_freq * radian_freq * (1.0 / GRAVITY)
        growths.append(radian_freq)
        keeps.append(active / (1.0 + decay * wavenum))

    @pl.loop(0, dir_count)
    def _(j):
        up = lax.rem(j + 3, dir_count)
        back = lax.rem(j + dir_count - 1, dir_count)
        wind = tab_ref[4 * dir_count + j] * wind_ref[0] + tab_ref[5 * dir_count + j] * wind_ref[1]
        for index in range(local_bands):
            radian_freq = growths[index]
            quad = delta_ref[index, back] + delta_ref[index + 2, up] - 2.0 * delta_ref[index + 1, j]
            gain = 1.0 + jnp.maximum(radian_freq * wind - 1.0, 0.0) * (WIND_COEF * radian_freq)
            out_ref[index, j] = density(index, j) * gain * keeps[index] + quad * quad_scale


def source(strip, shape, band_total, pos, table, land_sea, wind, sums, sum_block, own, below, above, choosers, previous):
    local_bands, dir_count, row_count, cols = shape
    spill_count = len(choosers)
    lane_grid = cols // LANES
    smem = pl.BlockSpec(memory_space=pltpu.SMEM)
    part = lambda ref: pl.BlockSpec((ref.shape[0], dir_count, STRIP, LANES), lambda c: (0, 0, 0, c))
    full = lambda ref: pl.BlockSpec(ref.shape, lambda c: (0,) * ref.ndim)
    in_specs = [smem, smem]
    in_specs.append(pl.BlockSpec((STRIP, LANES), lambda c: (strip, c)))
    in_specs.append(pl.BlockSpec((2, STRIP, LANES), lambda c: (0, strip, c)))
    in_specs.append(pl.BlockSpec((2, STRIP, LANES), lambda c: (0, sum_block, c)))
    in_specs += [part(ref) for ref in own]
    in_specs += [full(ref) if spill_count else part(ref) for ref in below + above]
    in_specs += [pl.BlockSpec((LANES, cols), lambda c: (c, 0))] * spill_count
    operands = [pos, table, land_sea, wind, sums, *own, *below, *above, *choosers]
    aliases = {}
    if previous is not None:
        in_specs.append(pl.BlockSpec(memory_space=pl.ANY))
        aliases = {len(operands): 0}
        operands.append(previous)
    scratch = [pltpu.VMEM((local_bands + 2, dir_count, STRIP, LANES), jnp.float32)]
    sides = (len(below) // max(spill_count, 1), len(above) // max(spill_count, 1))
    if spill_count:
        scratch.append(pltpu.VMEM((3 * dir_count * STRIP, cols), jnp.bfloat16))
        scratch.append(pltpu.VMEM((4, dir_count, STRIP, LANES), jnp.float32))
    cells = local_bands * dir_count * STRIP * cols
    return pl.pallas_call(
        functools.partial(
            source_kernel, strip, band_total, dir_count, local_bands, len(own), sides[0], sides[1], spill_count, previous is None
        ),
        grid=(lane_grid,),
        in_specs=in_specs,
        out_specs=pl.BlockSpec((local_bands, dir_count, STRIP, LANES), lambda c: (0, 0, strip, c)),
        out_shape=jax.ShapeDtypeStruct(shape, jnp.float32),
        scratch_shapes=scratch,
        input_output_aliases=aliases,
        compiler_params=pltpu.CompilerParams(vmem_limit_bytes=VMEM_BYTES),
        cost_estimate=pl.CostEstimate(flops=30 * cells, bytes_accessed=16 * cells, transcendentals=0),
        name="source",
    )(*operands)


def shards(spectrum, land_sea, sea_index, sea_count, wind_speed, wind_dir, slope_x, slope_y):
    local_bands, dir_count, row_count, cols = spectrum.shape
    spec_count = lax.axis_size("spec")
    geo_count = lax.axis_size("geo")
    band_total = local_bands * spec_count
    pos = lax.axis_index("spec").astype(jnp.int32).reshape(1)
    table = jnp.asarray(tables(band_total, dir_count))
    inner, outer, spill = (1, 2), (0, 3), 2
    choose = plan(land_sea, (1, 0, 3), spill)
    size = min(2, local_bands)
    groups = list(range(0, local_bands, size))

    args = (band_total, pos, table, spectrum, land_sea, slope_x, slope_y)
    cells = {s: [] for s in range(4)}
    sends = {1: [], 0: [], 3: []}
    inner_sums, outer_sums = [], []
    for group in groups:
        strip_a, strip_b, send, sums, head, tail = propagate(
            inner, 1, (0,), False, group, size, *args, (), choose[:1]
        )
        cells[1].append(strip_a)
        cells[2].append(strip_b)
        sends[1].append(send)
        inner_sums.append((sums, head, tail))
    ups = [(i, i + 1) for i in range(geo_count - 1)]
    downs = [(i + 1, i) for i in range(geo_count - 1)]
    for index, group in enumerate(groups):
        _, head, tail = inner_sums[index]
        lower = lax.ppermute(tail, "geo", ups)
        upper = lax.ppermute(head, "geo", downs)
        strip_a, strip_b, send_a, send_b, sums = propagate(
            outer, None, (0, 1), True, group, size, *args, (lower, upper, cells[2][index]), choose[1:]
        )
        cells[0].append(strip_a)
        cells[3].append(strip_b)
        sends[0].append(send_a)
        sends[3].append(send_b)
        outer_sums.append(sums)
    total_inner = functools.reduce(jnp.add, [entry[0] for entry in inner_sums])
    total_outer = functools.reduce(jnp.add, outer_sums)
    sums = lax.psum(jnp.concatenate([total_inner, total_outer], axis=1), "spec")

    def hop(value, count):
        pairs = [(i, i + count) for i in range(spec_count) if 0 <= i + count < spec_count]
        return lax.ppermute(value, "spec", pairs)

    below, above = {}, {}
    for s in (1, 0, 3):
        if size == 2:
            below[s] = [hop(sends[s][-1], 1)]
            above[s] = [hop(sends[s][0], -1)]
        else:
            below[s] = [hop(sends[s][0], 2), hop(sends[s][0], 1)]
            above[s] = [hop(sends[s][0], -1), hop(sends[s][0], -2)]

    scale = (28.0 * USTAR_RATIO / GRAVITY) * wind_speed
    wind = jnp.stack([scale * jnp.cos(wind_dir), scale * jnp.sin(wind_dir)])
    result = None
    sum_block = {1: 0, 2: 1, 0: 2, 3: 3}
    for s in (1, 0, 3):
        result = source(
            s, spectrum.shape, band_total, pos, table, land_sea, wind, sums, sum_block[s], cells[s], below[s], above[s], [], result
        )
    all_below = [ref for s in (1, 0, 3) for ref in below[s]]
    all_above = [ref for s in (1, 0, 3) for ref in above[s]]
    return source(
        spill, spectrum.shape, band_total, pos, table, land_sea, wind, sums, sum_block[spill], cells[spill], all_below, all_above, list(choose), result
    )


def solution(mesh):
    placed = (
        P("spec", None, "geo", None),
        P("geo", None),
        P("geo", None),
        P("geo"),
        P("geo", None),
        P("geo", None),
        P("geo", None),
        P("geo", None),
    )
    return jax.shard_map(
        shards, mesh=mesh, in_specs=placed, out_specs=P("spec", None, "geo", None), check_vma=False
    )
```

```python
import functools
import math

import jax
import jax.numpy as jnp
import numpy as np
from jax import lax
from jax.experimental import pallas as pl
from jax.experimental.pallas import tpu as pltpu
from jax.sharding import PartitionSpec as P

GRAVITY = 9.81
BASE_FREQ = 0.035
GROWTH = 1.1
COURANT_TOP = 0.9
TURN_TOP = 1.2
SPACING = 0.1
USTAR_RATIO = 0.035
WIND_COEF = 0.0375
WHITECAP = 0.36
STEEP_REF = 1.6
EPSILON = 1e-06
QUAD_COEF = 100.0

STRIP = 8
LANES = 128
VMEM_BYTES = 56 * 1024 * 1024
ROW_UNROLL = 9
TURN_UNROLL = 3
DELTA_UNROLL = 4
SOURCE_UNROLL = 4


def tables(band_total, dir_count):
    dtheta = 2.0 * math.pi / dir_count
    angles = (np.arange(dir_count) + 0.5) * dtheta
    faces = np.arange(dir_count) * dtheta
    parts = [
        np.abs(np.cos(angles)),
        np.abs(np.sin(angles)),
        np.sin(faces),
        np.cos(faces),
        np.cos(angles),
        np.sin(angles),
        GROWTH ** np.arange(band_total),
    ]
    return np.concatenate(parts).astype(np.float32)


def sign_runs(dir_count):
    angles = (np.arange(dir_count) + 0.5) * 2.0 * math.pi / dir_count
    signs = [(bool(np.cos(a) >= 0), bool(np.sin(a) >= 0)) for a in angles]
    runs, first = [], 0
    for j in range(1, dir_count + 1):
        if j == dir_count or signs[j] != signs[first]:
            runs.append((first, j) + signs[first])
            first = j
    return runs


def unrolled(first, last, count):
    def wrap(body):
        turns = (last - first) // count
        if turns:

            @pl.loop(0, turns)
            def _(turn):
                for k in range(count):
                    body(first + turn * count + k)

        for j in range(first + turns * count, last):
            body(j)

    return wrap


def plan_kernel(kept, spill, wanted, back, land_ref, *out_refs):
    cols = land_ref.shape[1]
    flags = [land_ref[STRIP * s : STRIP * s + 1, :].astype(jnp.float32) for s in (spill,) + tuple(kept)]
    rows = [flags[0]] + [1.0 - flag for flag in flags[1:]]
    rows += [jnp.zeros((1, cols), jnp.float32)] * (8 - len(rows))
    table = jnp.concatenate(rows, axis=0)
    first = lax.broadcasted_iota(jnp.int32, (cols, cols), 0)
    second = lax.broadcasted_iota(jnp.int32, (cols, cols), 1)
    block = STRIP
    starts = lax.broadcasted_iota(jnp.int32, (8, cols), 1) % block == 0
    narrow = jnp.where(starts, table, 0.0).astype(jnp.bfloat16)
    before = jnp.where(first < (second & ~(block - 1)), 1.0, 0.0).astype(jnp.bfloat16)
    ranks = jnp.dot(narrow, before, preferred_element_type=jnp.float32)
    phase = (first & (block - 1)) == (second & (block - 1))
    marks = [jnp.where(table[0:1] > 0.5, ranks[0:1], -1.0)]
    offset = jnp.zeros((1, 1), jnp.float32)
    for index in range(len(kept)):
        hole = table[index + 1 : index + 2, :]
        marks.append(jnp.where(hole > 0.5, ranks[index + 1 : index + 2, :] + offset, -2.0))
        offset = offset + jnp.sum(hole, axis=1, keepdims=True) * (1.0 / block)
    marks = jnp.concatenate(marks + [jnp.zeros((1, cols), jnp.float32)] * (8 - len(marks)), axis=0)
    columns = marks.T
    for index, out_ref in zip(wanted, out_refs):
        if back:
            match = jnp.abs(columns[:, index + 1 : index + 2] - marks[0:1, :]) < 0.5
        else:
            match = jnp.abs(columns[:, 0:1] - marks[index + 1 : index + 2, :]) < 0.5
        out_ref[...] = jnp.where(jnp.logical_and(phase, match), 1.0, 0.0).astype(jnp.bfloat16)


def plan(land_sea, kept, spill, wanted, back):
    cols = land_sea.shape[1]
    return pl.pallas_call(
        functools.partial(plan_kernel, kept, spill, wanted, back),
        out_shape=[jax.ShapeDtypeStruct((cols, cols), jnp.bfloat16)] * len(wanted),
        compiler_params=pltpu.CompilerParams(vmem_limit_bytes=VMEM_BYTES),
        name="plan_back" if back else "plan",
    )(land_sea)


def taps(courant):
    rest = (1.0 - courant * courant) * (1.0 / 6.0)
    down = courant * (0.5 - 0.5 * courant - rest)
    centre = courant * (0.5 + 0.5 * courant + 2.0 * rest)
    far = -courant * rest
    return -down, 1.0 - centre + down, centre - far, far


def row_shift(before, cells, after, shift, row_ids):
    if shift > 0:
        return jnp.where(row_ids < shift, pltpu.roll(before, shift, 0), pltpu.roll(cells, shift, 0))
    count = cells.shape[0]
    return jnp.where(
        row_ids >= count + shift, pltpu.roll(after, count + shift, 0), pltpu.roll(cells, count + shift, 0)
    )


def lane_shift(pieces, shift, lane_ids):
    rolled = [pltpu.roll(piece, shift % LANES, 1) for piece in pieces]
    zero = jnp.zeros_like(pieces[0])
    moved = []
    for index in range(len(pieces)):
        if shift > 0:
            other = rolled[index - 1] if index > 0 else zero
            moved.append(jnp.where(lane_ids < shift, other, rolled[index]))
        else:
            other = rolled[index + 1] if index + 1 < len(pieces) else zero
            moved.append(jnp.where(lane_ids >= LANES + shift, other, rolled[index]))
    return moved


def exact_dot(cells, chooser, split_ref):
    count = cells.shape[0]
    high = cells.astype(jnp.bfloat16)
    rest = cells - high.astype(jnp.float32)
    mid = rest.astype(jnp.bfloat16)
    low = (rest - mid.astype(jnp.float32)).astype(jnp.bfloat16)
    split_ref[0:count, :] = high
    split_ref[count : 2 * count, :] = mid
    split_ref[2 * count : 3 * count, :] = low
    product = jnp.dot(split_ref[...], chooser, preferred_element_type=jnp.float32)
    return product[0:count] + product[count : 2 * count] + product[2 * count : 3 * count]


def propagate_kernel(strips, spill_slot, dests, edge, group, band_total, dir_count, local_bands, *refs):
    refs = list(refs)
    pos_ref, tab_ref, spec_ref, land_ref, sx_ref, sy_ref = refs[:6]
    refs = refs[6:]
    lower_ref = upper_ref = spill_ref = None
    if edge:
        lower_ref, upper_ref, spill_ref = refs[:3]
        refs = refs[3:]
    choosers = refs[: len(dests)]
    refs = refs[len(dests) :]
    out_refs = refs[: len(strips)]
    refs = refs[len(strips) :]
    send_refs = refs[: len(dests)]
    refs = refs[len(dests) :]
    sum_ref = refs[0]
    refs = refs[1:]
    head_ref = tail_ref = None
    if not edge:
        head_ref, tail_ref = refs[:2]
        refs = refs[2:]
    turn_ref, moved_ref, split_ref = refs

    row_count, cols = land_ref.shape
    step = pl.program_id(0)
    band = pos_ref[0] * local_bands + group + step
    growth = tab_ref[6 * dir_count + band]
    courant = COURANT_TOP / growth
    turn_rate = TURN_TOP / growth
    radian_freq = (2.0 * math.pi * BASE_FREQ) * growth
    weight = SPACING * radian_freq * (2.0 * math.pi / dir_count)
    row_ids = lax.broadcasted_iota(jnp.int32, (STRIP, cols), 0)
    lane_ids = lax.broadcasted_iota(jnp.int32, (STRIP, LANES), 1)

    def wet(s):
        return land_ref[STRIP * s : STRIP * (s + 1), :].astype(jnp.float32)

    @pl.when(step == 0)
    def _():
        sum_ref[...] = jnp.zeros_like(sum_ref)

        @pl.loop(0, dir_count)
        def _(f):
            face_sin = tab_ref[2 * dir_count + f]
            face_cos = tab_ref[3 * dir_count + f]
            for slot, s in enumerate(strips):
                rows = slice(STRIP * s, STRIP * (s + 1))
                turn_ref[slot, f] = face_sin * sx_ref[rows, :] - face_cos * sy_ref[rows, :]

    if not edge:
        wet_head = land_ref[0:2, :].astype(jnp.float32)
        wet_tail = land_ref[row_count - 2 : row_count, :].astype(jnp.float32)

    for first, last, cos_up, sin_up in sign_runs(dir_count):

        @unrolled(first, last, ROW_UNROLL)
        def _(j):
            row_taps = taps(courant * tab_ref[j])
            col_taps = taps(courant * tab_ref[dir_count + j])
            if not edge:
                head_ref[0, j] = spec_ref[0, j, 0:2, :] * wet_head
                tail_ref[0, j] = spec_ref[0, j, row_count - 2 : row_count, :] * wet_tail
            for slot, s in enumerate(strips):
                wet_s = wet(s)
                cells = spec_ref[0, j, STRIP * s : STRIP * (s + 1), :] * wet_s
                if s == 0:
                    before = jnp.concatenate(
                        [jnp.zeros((STRIP - 2, cols), jnp.float32), lower_ref[0, j]], axis=0
                    )
                else:
                    before = spec_ref[0, j, STRIP * (s - 1) : STRIP * s, :] * wet(s - 1)
                if STRIP * (s + 1) == row_count:
                    after = jnp.concatenate(
                        [upper_ref[0, j], jnp.zeros((STRIP - 2, cols), jnp.float32)], axis=0
                    )
                else:
                    after = spec_ref[0, j, STRIP * (s + 1) : STRIP * (s + 2), :] * wet(s + 1)
                way = 1 if cos_up else -1
                cells = (
                    row_taps[1] * cells
                    + row_taps[0] * row_shift(before, cells, after, -way, row_ids)
                    + row_taps[2] * row_shift(before, cells, after, way, row_ids)
                    + row_taps[3] * row_shift(before, cells, after, 2 * way, row_ids)
                ) * wet_s
                way = 1 if sin_up else -1
                pieces = [cells[:, LANES * c : LANES * (c + 1)] for c in range(cols // LANES)]
                down = lane_shift(pieces, -way, lane_ids)
                upwind = lane_shift(pieces, way, lane_ids)
                far = lane_shift(pieces, 2 * way, lane_ids)
                for c in range(cols // LANES):
                    lanes = slice(LANES * c, LANES * (c + 1))
                    moved_ref[slot, j + 2, :, lanes] = (
                        col_taps[1] * pieces[c]
                        + col_taps[0] * down[c]
                        + col_taps[2] * upwind[c]
                        + col_taps[3] * far[c]
                    ) * wet_s[:, lanes]

    moved_ref[:, 0:2] = moved_ref[:, dir_count : dir_count + 2]
    moved_ref[:, dir_count + 2 : dir_count + 4] = moved_ref[:, 2:4]

    def face_flux(slot, f, turning):
        far_left, left = moved_ref[slot, f], moved_ref[slot, f + 1]
        right, far_right = moved_ref[slot, f + 2], moved_ref[slot, f + 3]
        rate = turn_rate * turning
        square = rate * rate
        slope = right - left
        bend = jnp.where(rate >= 0, slope - (left - far_left), (far_right - right) - slope)
        return rate * (
            0.5 * ((left + right) - rate * slope) - (1.0 / 6.0 - square * (1.0 / 6.0)) * bend
        )

    def turn(step, carry):
        carry = list(carry)
        for k in range(TURN_UNROLL):
            f = step * TURN_UNROLL + k + 1
            face = f if k < TURN_UNROLL - 1 else lax.rem(f, dir_count)
            for slot in range(len(strips)):
                lower, total = carry[slot]
                flux = face_flux(slot, f, turn_ref[slot, face])
                cell = jnp.maximum(moved_ref[slot, f + 1] - (flux - lower), 0.0)
                out_refs[slot][0, f - 1] = cell
                carry[slot] = (flux, total + cell)
        return tuple(carry)

    zero = jnp.zeros((STRIP, cols), jnp.float32)
    start = tuple((face_flux(slot, 0, turn_ref[slot, 0]), zero) for slot in range(len(strips)))
    ends = lax.fori_loop(0, dir_count // TURN_UNROLL, turn, start)
    for slot, (_, total) in enumerate(ends):
        rows = slice(STRIP * slot, STRIP * (slot + 1))
        sum_ref[0, rows, :] += weight * total
        sum_ref[1, rows, :] += (SPACING * 2.0 * math.pi / dir_count) * total

    source = spill_ref if edge else out_refs[spill_slot]
    spill = source[0].reshape(dir_count * STRIP, cols)
    for chooser, dest, send_ref in zip(choosers, dests, send_refs):
        filled = exact_dot(spill, chooser[...], split_ref)
        send_ref[0] = out_refs[dest][0] + filled.reshape(dir_count, STRIP, cols)


def propagate(strips, spill_slot, dests, edge, group, size, band_total, pos, table, spectrum, land_sea, slope_x, slope_y, extra, choosers):
    local_bands, dir_count, row_count, cols = spectrum.shape
    whole = lambda shape: pl.BlockSpec(shape, lambda b: (0,) * len(shape))
    one = lambda rows: pl.BlockSpec((1, dir_count, rows, cols), lambda b: (b, 0, 0, 0))
    smem = pl.BlockSpec(memory_space=pltpu.SMEM)
    flat = whole((row_count, cols))
    in_specs = [smem, smem]
    in_specs += [pl.BlockSpec((1, dir_count, row_count, cols), lambda b: (b + group, 0, 0, 0))]
    in_specs += [flat, flat, flat]
    if edge:
        halo = pl.BlockSpec((1, dir_count, 2, cols), lambda b: (b, 0, 0, 0))
        in_specs += [halo, halo, one(STRIP)]
    in_specs += [whole((cols, cols))] * len(choosers)
    band_array = lambda rows: jax.ShapeDtypeStruct((size, dir_count, rows, cols), jnp.float32)
    out_shape = [band_array(STRIP)] * (len(strips) + len(dests))
    out_specs = [one(STRIP)] * (len(strips) + len(dests))
    sums = (2, STRIP * len(strips), cols)
    out_shape.append(jax.ShapeDtypeStruct(sums, jnp.float32))
    out_specs.append(whole(sums))
    if not edge:
        out_shape += [band_array(2)] * 2
        out_specs += [one(2)] * 2
    cells = size * dir_count * len(strips) * STRIP * cols
    return pl.pallas_call(
        functools.partial(
            propagate_kernel, strips, spill_slot, dests, edge, group, band_total, dir_count, local_bands
        ),
        grid=(size,),
        in_specs=in_specs,
        out_specs=out_specs,
        out_shape=out_shape,
        scratch_shapes=[
            pltpu.VMEM((len(strips), dir_count, STRIP, cols), jnp.float32),
            pltpu.VMEM((len(strips), dir_count + 4, STRIP, cols), jnp.float32),
            pltpu.VMEM((3 * dir_count * STRIP, cols), jnp.bfloat16),
        ],
        compiler_params=pltpu.CompilerParams(vmem_limit_bytes=VMEM_BYTES),
        cost_estimate=pl.CostEstimate(flops=60 * cells, bytes_accessed=16 * cells, transcendentals=0),
        name="propagate_edge" if edge else "propagate_inner",
    )(pos, table, spectrum, land_sea, slope_x, slope_y, *extra, *choosers)


def unpack_kernel(has_total, send_ref, chooser_ref, *refs):
    out_ref, split_ref = refs[-2:]
    _, dir_count, rows, cols = send_ref.shape
    cells = exact_dot(send_ref[0].reshape(dir_count * rows, cols), chooser_ref[...], split_ref)
    cells = cells.reshape(dir_count, rows, cols)
    out_ref[0] = cells + refs[0][0] if has_total else cells


def unpack(sent, chooser, total):
    bands, dir_count, rows, cols = sent.shape
    one = pl.BlockSpec((1, dir_count, rows, cols), lambda b: (b, 0, 0, 0))
    totals = [] if total is None else [total]
    return pl.pallas_call(
        functools.partial(unpack_kernel, total is not None),
        grid=(bands,),
        in_specs=[one, pl.BlockSpec(chooser.shape, lambda b: (0, 0))] + [one] * len(totals),
        out_specs=one,
        out_shape=jax.ShapeDtypeStruct(sent.shape, jnp.float32),
        scratch_shapes=[pltpu.VMEM((3 * dir_count * rows, cols), jnp.bfloat16)],
        compiler_params=pltpu.CompilerParams(vmem_limit_bytes=VMEM_BYTES),
        cost_estimate=pl.CostEstimate(flops=8 * sent.size, bytes_accessed=12 * sent.size, transcendentals=0),
        name="unpack",
    )(sent, chooser, *totals)


def source_kernel(dir_count, local_bands, group_count, below_count, above_count, *refs):
    pos_ref, tab_ref, land_ref, wind_ref, sum_ref = refs[:5]
    refs = refs[5:]
    own = refs[:group_count]
    below = refs[group_count : group_count + below_count]
    above = refs[group_count + below_count : group_count + below_count + above_count]
    out_ref, delta_ref = refs[-2:]
    bands = [(ref, i) for ref in (*below, *own, *above) for i in range(ref.shape[0])]

    def density(index, j):
        ref, slot = bands[index + 2]
        return ref[slot, j]

    energy = sum_ref[0] + EPSILON
    first_sum = sum_ref[1]
    mean_sigma = energy / (first_sum + EPSILON)
    ratio = energy / (math.sqrt(GRAVITY) * first_sum + EPSILON)
    mean_k = ratio * ratio
    steepness = energy * mean_k * mean_k / STEEP_REF
    decay = WHITECAP * mean_sigma / mean_k * steepness * steepness
    active = land_ref[...].astype(jnp.float32)
    quad_scale = active * QUAD_COEF / (energy * energy)

    @unrolled(0, dir_count, DELTA_UNROLL)
    def _(j):
        up = lax.rem(j + 1, dir_count)
        back = lax.rem(j + dir_count - 3, dir_count)
        for index in range(-1, local_bands + 1):
            center = density(index, j)
            plus = density(index + 1, up)
            minus = density(index - 1, back)
            delta_ref[index + 1, j] = center * (center * (plus + minus) - 2.0 * (plus * minus))

    growths, keeps = [], []
    for index in range(local_bands):
        growth = tab_ref[6 * dir_count + pos_ref[0] * local_bands + index]
        radian_freq = (2.0 * math.pi * BASE_FREQ) * growth
        wavenum = radian_freq * radian_freq * (1.0 / GRAVITY)
        growths.append(radian_freq)
        keeps.append(active / (1.0 + decay * wavenum))

    @unrolled(0, dir_count, SOURCE_UNROLL)
    def _(j):
        up = lax.rem(j + 3, dir_count)
        back = lax.rem(j + dir_count - 1, dir_count)
        wind = tab_ref[4 * dir_count + j] * wind_ref[0] + tab_ref[5 * dir_count + j] * wind_ref[1]
        for index in range(local_bands):
            radian_freq = growths[index]
            quad = delta_ref[index, back] + delta_ref[index + 2, up] - 2.0 * delta_ref[index + 1, j]
            gain = 1.0 + jnp.maximum(radian_freq * wind - 1.0, 0.0) * (WIND_COEF * radian_freq)
            out_ref[index, j] = density(index, j) * gain * keeps[index] + quad * quad_scale


def source(strip, shape, pos, table, land_sea, wind, sums, sum_block, own, below, above, previous):
    local_bands, dir_count, row_count, cols = shape
    smem = pl.BlockSpec(memory_space=pltpu.SMEM)
    part = lambda ref: pl.BlockSpec((ref.shape[0], dir_count, STRIP, LANES), lambda c: (0, 0, 0, c))
    in_specs = [smem, smem]
    in_specs.append(pl.BlockSpec((STRIP, LANES), lambda c: (strip, c)))
    in_specs.append(pl.BlockSpec((2, STRIP, LANES), lambda c: (0, strip, c)))
    in_specs.append(pl.BlockSpec((2, STRIP, LANES), lambda c: (0, sum_block, c)))
    in_specs += [part(ref) for ref in own + below + above]
    operands = [pos, table, land_sea, wind, sums, *own, *below, *above]
    aliases = {}
    if previous is not None:
        in_specs.append(pl.BlockSpec(memory_space=pl.ANY))
        aliases = {len(operands): 0}
        operands.append(previous)
    cells = local_bands * dir_count * STRIP * cols
    return pl.pallas_call(
        functools.partial(source_kernel, dir_count, local_bands, len(own), len(below), len(above)),
        grid=(cols // LANES,),
        in_specs=in_specs,
        out_specs=pl.BlockSpec((local_bands, dir_count, STRIP, LANES), lambda c: (0, 0, strip, c)),
        out_shape=jax.ShapeDtypeStruct(shape, jnp.float32),
        scratch_shapes=[pltpu.VMEM((local_bands + 2, dir_count, STRIP, LANES), jnp.float32)],
        input_output_aliases=aliases,
        compiler_params=pltpu.CompilerParams(vmem_limit_bytes=VMEM_BYTES),
        cost_estimate=pl.CostEstimate(flops=30 * cells, bytes_accessed=16 * cells, transcendentals=0),
        name="source",
    )(*operands)


def spec_total(value):
    count = lax.axis_size("spec")
    if count & (count - 1):
        return lax.psum(value, "spec")
    reach = 1
    while reach < count:
        value = value + lax.ppermute(value, "spec", [(i, i ^ reach) for i in range(count)])
        reach *= 2
    return value


def shards(spectrum, land_sea, sea_index, sea_count, wind_speed, wind_dir, slope_x, slope_y):
    local_bands, dir_count, row_count, cols = spectrum.shape
    spec_count = lax.axis_size("spec")
    geo_count = lax.axis_size("geo")
    band_total = local_bands * spec_count
    pos = lax.axis_index("spec").astype(jnp.int32).reshape(1)
    table = jnp.asarray(tables(band_total, dir_count))
    inner, outer, spill = (1, 2), (0, 3), 2
    kept = (1, 0, 3)
    choose = plan(land_sea, kept, spill, (0,), False)
    size = min(2, local_bands)
    groups = list(range(0, local_bands, size))

    args = (band_total, pos, table, spectrum, land_sea, slope_x, slope_y)
    cells = {s: [] for s in range(4)}
    sends = {1: [], 0: [], 3: []}
    inner_sums, outer_sums = [], []
    for group in groups:
        strip_a, strip_b, send, sums, head, tail = propagate(
            inner, 1, (0,), False, group, size, *args, (), choose[:1]
        )
        cells[1].append(strip_a)
        cells[2].append(strip_b)
        sends[1].append(send)
        inner_sums.append((sums, head, tail))
    choose = choose + plan(land_sea, kept, spill, (1, 2), False)
    ups = [(i, i + 1) for i in range(geo_count - 1)]
    downs = [(i + 1, i) for i in range(geo_count - 1)]
    for index, group in enumerate(groups):
        _, head, tail = inner_sums[index]
        lower = lax.ppermute(tail, "geo", ups)
        upper = lax.ppermute(head, "geo", downs)
        strip_a, strip_b, send_a, send_b, sums = propagate(
            outer, None, (0, 1), True, group, size, *args, (lower, upper, cells[2][index]), choose[1:]
        )
        cells[0].append(strip_a)
        cells[3].append(strip_b)
        sends[0].append(send_a)
        sends[3].append(send_b)
        outer_sums.append(sums)
    inner_total = spec_total(functools.reduce(jnp.add, [entry[0] for entry in inner_sums]))
    outer_total = spec_total(functools.reduce(jnp.add, outer_sums))

    def hop(value, count):
        pairs = [(i, i + count) for i in range(spec_count) if 0 <= i + count < spec_count]
        return lax.ppermute(value, "spec", pairs)

    below, above = {}, {}
    for s in kept:
        if size == 2:
            below[s] = [hop(sends[s][-1], 1)]
            above[s] = [hop(sends[s][0], -1)]
        else:
            below[s] = [hop(sends[s][0], 2), hop(sends[s][0], 1)]
            above[s] = [hop(sends[s][0], -1), hop(sends[s][0], -2)]

    scale = (28.0 * USTAR_RATIO / GRAVITY) * wind_speed
    wind = jnp.stack([scale * jnp.cos(wind_dir), scale * jnp.sin(wind_dir)])
    back = plan(land_sea, kept, spill, (0, 1, 2), True)
    below[spill], above[spill] = [None] * len(below[1]), [None] * len(above[1])
    for s, chooser in zip(kept, back):
        for side in (below, above):
            side[spill] = [unpack(sent, chooser, total) for sent, total in zip(side[s], side[spill])]
    result = None
    for s in kept + (spill,):
        sums, block = (inner_total, inner.index(s)) if s in inner else (outer_total, outer.index(s))
        result = source(
            s, spectrum.shape, pos, table, land_sea, wind, sums, block, cells[s], below[s], above[s], result
        )
    return result


def solution(mesh):
    placed = (
        P("spec", None, "geo", None),
        P("geo", None),
        P("geo", None),
        P("geo"),
        P("geo", None),
        P("geo", None),
        P("geo", None),
        P("geo", None),
    )
    return jax.shard_map(
        shards, mesh=mesh, in_specs=placed, out_specs=P("spec", None, "geo", None), check_vma=False
    )
```

```python
import functools
import math

import jax
import jax.numpy as jnp
import numpy as np
from jax import lax
from jax.experimental import pallas as pl
from jax.experimental.pallas import tpu as pltpu
from jax.sharding import PartitionSpec as P

GRAVITY = 9.81
BASE_FREQ = 0.035
GROWTH = 1.1
COURANT_TOP = 0.9
TURN_TOP = 1.2
SPACING = 0.1
USTAR_RATIO = 0.035
WIND_COEF = 0.0375
WHITECAP = 0.36
STEEP_REF = 1.6
EPSILON = 1e-06
QUAD_COEF = 100.0

STRIP = 8
LANES = 128
VMEM_BYTES = 56 * 1024 * 1024
ROW_UNROLL = 9
TURN_UNROLL = 3
DELTA_UNROLL = 4
SOURCE_UNROLL = 4
SOURCE_LANES = 256
COST = pl.CostEstimate(flops=1024, bytes_accessed=1024, transcendentals=0)


def tables(band_total, dir_count):
    dtheta = 2.0 * math.pi / dir_count
    angles = (np.arange(dir_count) + 0.5) * dtheta
    faces = np.arange(dir_count) * dtheta
    parts = [
        np.abs(np.cos(angles)),
        np.abs(np.sin(angles)),
        np.sin(faces),
        np.cos(faces),
        np.cos(angles),
        np.sin(angles),
        GROWTH ** np.arange(band_total),
    ]
    return np.concatenate(parts).astype(np.float32)


def sign_runs(dir_count):
    angles = (np.arange(dir_count) + 0.5) * 2.0 * math.pi / dir_count
    signs = [(bool(np.cos(a) >= 0), bool(np.sin(a) >= 0)) for a in angles]
    runs, first = [], 0
    for j in range(1, dir_count + 1):
        if j == dir_count or signs[j] != signs[first]:
            runs.append((first, j) + signs[first])
            first = j
    return runs


def unrolled(first, last, count):
    def wrap(body):
        turns = (last - first) // count
        if turns:

            @pl.loop(0, turns)
            def _(turn):
                for k in range(count):
                    body(first + turn * count + k)

        for j in range(first + turns * count, last):
            body(j)

    return wrap


def plan_kernel(kept, spill, wanted, back, land_ref, *out_refs):
    cols = land_ref.shape[1]
    flags = [land_ref[STRIP * s : STRIP * s + 1, :].astype(jnp.float32) for s in (spill,) + tuple(kept)]
    rows = [flags[0]] + [1.0 - flag for flag in flags[1:]]
    rows += [jnp.zeros((1, cols), jnp.float32)] * (8 - len(rows))
    table = jnp.concatenate(rows, axis=0)
    first = lax.broadcasted_iota(jnp.int32, (cols, cols), 0)
    second = lax.broadcasted_iota(jnp.int32, (cols, cols), 1)
    block = STRIP
    starts = lax.broadcasted_iota(jnp.int32, (8, cols), 1) % block == 0
    narrow = jnp.where(starts, table, 0.0).astype(jnp.bfloat16)
    before = jnp.where(first < (second & ~(block - 1)), 1.0, 0.0).astype(jnp.bfloat16)
    ranks = jnp.dot(narrow, before, preferred_element_type=jnp.float32)
    phase = (first & (block - 1)) == (second & (block - 1))
    marks = [jnp.where(table[0:1] > 0.5, ranks[0:1], -1.0)]
    offset = jnp.zeros((1, 1), jnp.float32)
    for index in range(len(kept)):
        hole = table[index + 1 : index + 2, :]
        marks.append(jnp.where(hole > 0.5, ranks[index + 1 : index + 2, :] + offset, -2.0))
        offset = offset + jnp.sum(hole, axis=1, keepdims=True) * (1.0 / block)
    marks = jnp.concatenate(marks + [jnp.zeros((1, cols), jnp.float32)] * (8 - len(marks)), axis=0)
    columns = marks.T
    for index, out_ref in zip(wanted, out_refs):
        if back:
            match = jnp.abs(columns[:, index + 1 : index + 2] - marks[0:1, :]) < 0.5
        else:
            match = jnp.abs(columns[:, 0:1] - marks[index + 1 : index + 2, :]) < 0.5
        out_ref[...] = jnp.where(jnp.logical_and(phase, match), 1.0, 0.0).astype(jnp.bfloat16)


def plan(land_sea, kept, spill, wanted, back):
    cols = land_sea.shape[1]
    return pl.pallas_call(
        functools.partial(plan_kernel, kept, spill, wanted, back),
        out_shape=[jax.ShapeDtypeStruct((cols, cols), jnp.bfloat16)] * len(wanted),
        compiler_params=pltpu.CompilerParams(vmem_limit_bytes=VMEM_BYTES),
        name="plan_back" if back else "plan",
    )(land_sea)


def taps(courant):
    rest = (1.0 - courant * courant) * (1.0 / 6.0)
    down = courant * (0.5 - 0.5 * courant - rest)
    centre = courant * (0.5 + 0.5 * courant + 2.0 * rest)
    far = -courant * rest
    return -down, 1.0 - centre + down, centre - far, far


def row_shift(before, cells, after, shift, row_ids):
    if shift > 0:
        return jnp.where(row_ids < shift, pltpu.roll(before, shift, 0), pltpu.roll(cells, shift, 0))
    count = cells.shape[0]
    return jnp.where(
        row_ids >= count + shift, pltpu.roll(after, count + shift, 0), pltpu.roll(cells, count + shift, 0)
    )


def lane_shift(pieces, shift, lane_ids):
    rolled = [pltpu.roll(piece, shift % LANES, 1) for piece in pieces]
    zero = jnp.zeros_like(pieces[0])
    moved = []
    for index in range(len(pieces)):
        if shift > 0:
            other = rolled[index - 1] if index > 0 else zero
            moved.append(jnp.where(lane_ids < shift, other, rolled[index]))
        else:
            other = rolled[index + 1] if index + 1 < len(pieces) else zero
            moved.append(jnp.where(lane_ids >= LANES + shift, other, rolled[index]))
    return moved


def exact_dot(cells, chooser, split_ref):
    count = cells.shape[0]
    split_store(cells, split_ref)
    product = jnp.dot(split_ref[...], chooser, preferred_element_type=jnp.float32)
    return product[0:count] + product[count : 2 * count] + product[2 * count : 3 * count]


def split_store(cells, split_ref):
    count = cells.shape[0]
    high = cells.astype(jnp.bfloat16)
    rest = cells - high.astype(jnp.float32)
    mid = rest.astype(jnp.bfloat16)
    low = (rest - mid.astype(jnp.float32)).astype(jnp.bfloat16)
    split_ref[0:count, :] = high
    split_ref[count : 2 * count, :] = mid
    split_ref[2 * count : 3 * count, :] = low


def local_band(index, flip, local_bands):
    return index + flip * (local_bands - 1 - 2 * index)


def propagate_kernel(strips, spill_slot, dests, split, edge, chained, group, dir_count, local_bands, *refs):
    refs = list(refs)
    meta_ref, tab_ref, spec_ref, land_ref, sx_ref, sy_ref = refs[:6]
    refs = refs[6:]
    prior_ref = None
    if chained:
        prior_ref = refs[0]
        refs = refs[1:]
    lower_ref = upper_ref = spill_ref = None
    if edge:
        lower_ref, upper_ref, spill_ref = refs[:3]
        refs = refs[3:]
    choosers = refs[: len(dests)]
    refs = refs[len(dests) :]
    out_refs = refs[: len(strips)]
    refs = refs[len(strips) :]
    send_count = sum(2 if two else 1 for two in split)
    send_refs = refs[:send_count]
    refs = refs[send_count:]
    sum_ref = refs[0]
    refs = refs[1:]
    head_ref = tail_ref = None
    if not edge:
        head_ref, tail_ref = refs[:2]
        refs = refs[2:]
    turn_ref, moved_ref, split_ref = refs

    row_count, cols = land_ref.shape
    step = pl.program_id(0)
    band = meta_ref[0] * local_bands + local_band(group + step, meta_ref[1], local_bands)
    growth = tab_ref[6 * dir_count + band]
    courant = COURANT_TOP / growth
    turn_rate = TURN_TOP / growth
    radian_freq = (2.0 * math.pi * BASE_FREQ) * growth
    weight = SPACING * radian_freq * (2.0 * math.pi / dir_count)
    row_ids = lax.broadcasted_iota(jnp.int32, (STRIP, cols), 0)
    lane_ids = lax.broadcasted_iota(jnp.int32, (STRIP, LANES), 1)

    def wet(s):
        return land_ref[STRIP * s : STRIP * (s + 1), :].astype(jnp.float32)

    @pl.when(step == 0)
    def _():
        sum_ref[...] = prior_ref[...] if chained else jnp.zeros_like(sum_ref)

        @pl.loop(0, dir_count)
        def _(f):
            face_sin = tab_ref[2 * dir_count + f]
            face_cos = tab_ref[3 * dir_count + f]
            for slot, s in enumerate(strips):
                rows = slice(STRIP * s, STRIP * (s + 1))
                turn_ref[slot, f] = face_sin * sx_ref[rows, :] - face_cos * sy_ref[rows, :]

    if not edge:
        wet_head = land_ref[0:2, :].astype(jnp.float32)
        wet_tail = land_ref[row_count - 2 : row_count, :].astype(jnp.float32)

    for first, last, cos_up, sin_up in sign_runs(dir_count):

        @unrolled(first, last, ROW_UNROLL)
        def _(j):
            row_taps = taps(courant * tab_ref[j])
            col_taps = taps(courant * tab_ref[dir_count + j])
            if not edge:
                head_ref[0, j] = spec_ref[0, j, 0:2, :] * wet_head
                tail_ref[0, j] = spec_ref[0, j, row_count - 2 : row_count, :] * wet_tail
            for slot, s in enumerate(strips):
                wet_s = wet(s)
                cells = spec_ref[0, j, STRIP * s : STRIP * (s + 1), :] * wet_s
                if s == 0:
                    before = jnp.concatenate(
                        [jnp.zeros((STRIP - 2, cols), jnp.float32), lower_ref[0, j]], axis=0
                    )
                else:
                    before = spec_ref[0, j, STRIP * (s - 1) : STRIP * s, :] * wet(s - 1)
                if STRIP * (s + 1) == row_count:
                    after = jnp.concatenate(
                        [upper_ref[0, j], jnp.zeros((STRIP - 2, cols), jnp.float32)], axis=0
                    )
                else:
                    after = spec_ref[0, j, STRIP * (s + 1) : STRIP * (s + 2), :] * wet(s + 1)
                way = 1 if cos_up else -1
                cells = (
                    row_taps[1] * cells
                    + row_taps[0] * row_shift(before, cells, after, -way, row_ids)
                    + row_taps[2] * row_shift(before, cells, after, way, row_ids)
                    + row_taps[3] * row_shift(before, cells, after, 2 * way, row_ids)
                ) * wet_s
                way = 1 if sin_up else -1
                pieces = [cells[:, LANES * c : LANES * (c + 1)] for c in range(cols // LANES)]
                down = lane_shift(pieces, -way, lane_ids)
                upwind = lane_shift(pieces, way, lane_ids)
                far = lane_shift(pieces, 2 * way, lane_ids)
                for c in range(cols // LANES):
                    lanes = slice(LANES * c, LANES * (c + 1))
                    moved_ref[slot, j + 2, :, lanes] = (
                        col_taps[1] * pieces[c]
                        + col_taps[0] * down[c]
                        + col_taps[2] * upwind[c]
                        + col_taps[3] * far[c]
                    ) * wet_s[:, lanes]

    moved_ref[:, 0:2] = moved_ref[:, dir_count : dir_count + 2]
    moved_ref[:, dir_count + 2 : dir_count + 4] = moved_ref[:, 2:4]

    def face_flux(slot, f, turning):
        far_left, left = moved_ref[slot, f], moved_ref[slot, f + 1]
        right, far_right = moved_ref[slot, f + 2], moved_ref[slot, f + 3]
        rate = turn_rate * turning
        square = rate * rate
        slope = right - left
        bend = jnp.where(rate >= 0, slope - (left - far_left), (far_right - right) - slope)
        return rate * (
            0.5 * ((left + right) - rate * slope) - (1.0 / 6.0 - square * (1.0 / 6.0)) * bend
        )

    def turn(step, carry):
        carry = list(carry)
        for k in range(TURN_UNROLL):
            f = step * TURN_UNROLL + k + 1
            face = f if k < TURN_UNROLL - 1 else lax.rem(f, dir_count)
            for slot in range(len(strips)):
                lower, total = carry[slot]
                flux = face_flux(slot, f, turn_ref[slot, face])
                cell = jnp.maximum(moved_ref[slot, f + 1] - (flux - lower), 0.0)
                out_refs[slot][0, f - 1] = cell
                carry[slot] = (flux, total + cell)
        return tuple(carry)

    zero = jnp.zeros((STRIP, cols), jnp.float32)
    start = tuple((face_flux(slot, 0, turn_ref[slot, 0]), zero) for slot in range(len(strips)))
    ends = lax.fori_loop(0, dir_count // TURN_UNROLL, turn, start)
    for slot, (_, total) in enumerate(ends):
        rows = slice(STRIP * strips[slot], STRIP * (strips[slot] + 1))
        sum_ref[0, rows, :] += weight * total
        sum_ref[1, rows, :] += (SPACING * 2.0 * math.pi / dir_count) * total

    source = spill_ref if edge else out_refs[spill_slot]
    spill = source[0].reshape(dir_count * STRIP, cols)
    for chooser, dest, two in zip(choosers, dests, split):
        filled = exact_dot(spill, chooser[...], split_ref).reshape(dir_count, STRIP, cols)
        if two:
            for index in range(2):

                @pl.when(step == index)
                def _():
                    send_refs[index][0] = out_refs[dest][0] + filled

            send_refs = send_refs[2:]
        else:
            send_refs[0][0] = out_refs[dest][0] + filled
            send_refs = send_refs[1:]


def propagate(strips, spill_slot, dests, split, edge, group, size, meta, table, spectrum, land_sea, slope_x, slope_y, prior, extra, choosers):
    local_bands, dir_count, row_count, cols = spectrum.shape
    whole = lambda shape: pl.BlockSpec(shape, lambda b, meta: (0,) * len(shape))
    one = lambda rows: pl.BlockSpec((1, dir_count, rows, cols), lambda b, meta: (b, 0, 0, 0))
    flat = whole((row_count, cols))
    in_specs = [pl.BlockSpec(memory_space=pltpu.SMEM)]
    in_specs += [
        pl.BlockSpec(
            (1, dir_count, row_count, cols),
            lambda b, meta: (local_band(b + group, meta[1], local_bands), 0, 0, 0),
        )
    ]
    in_specs += [flat, flat, flat]
    sums = (2, row_count, cols)
    in_specs += [whole(sums)] * len(prior)
    if edge:
        in_specs += [one(2), one(2), one(STRIP)]
    in_specs += [whole((cols, cols))] * len(choosers)
    band_array = lambda rows: jax.ShapeDtypeStruct((size, dir_count, rows, cols), jnp.float32)
    out_shape = [band_array(STRIP)] * len(strips)
    out_specs = [one(STRIP)] * len(strips)
    for two in split:
        if two:
            out_shape += [jax.ShapeDtypeStruct((1, dir_count, STRIP, cols), jnp.float32)] * 2
            out_specs += [whole((1, dir_count, STRIP, cols))] * 2
        else:
            out_shape.append(band_array(STRIP))
            out_specs.append(one(STRIP))
    out_shape.append(jax.ShapeDtypeStruct(sums, jnp.float32))
    out_specs.append(whole(sums))
    if not edge:
        out_shape += [band_array(2)] * 2
        out_specs += [one(2)] * 2
    return pl.pallas_call(
        functools.partial(propagate_kernel, strips, spill_slot, dests, split, edge, len(prior) > 0, group, dir_count, local_bands),
        grid_spec=pltpu.PrefetchScalarGridSpec(
            num_scalar_prefetch=1,
            grid=(size,),
            in_specs=in_specs,
            out_specs=out_specs,
            scratch_shapes=[
                pltpu.VMEM((len(strips), dir_count, STRIP, cols), jnp.float32),
                pltpu.VMEM((len(strips), dir_count + 4, STRIP, cols), jnp.float32),
                pltpu.VMEM((3 * dir_count * STRIP, cols), jnp.bfloat16),
            ],
        ),
        out_shape=out_shape,
        compiler_params=pltpu.CompilerParams(vmem_limit_bytes=VMEM_BYTES),
        cost_estimate=COST,
        name="propagate_edge" if edge else "propagate_inner",
    )(meta, table, spectrum, land_sea, slope_x, slope_y, *prior, *extra, *choosers)


def unpack_kernel(places, has_total, *refs):
    out_ref, split_ref = refs[-2:]
    total_ref, chooser_ref = refs[-4], refs[-4 - has_total]
    _, dir_count, rows, cols = out_ref.shape
    count = dir_count * rows
    for slot, place in enumerate(places):

        @pl.when(pl.program_id(0) == slot)
        def _():
            split_store(refs[place][0].reshape(count, cols), split_ref)

    product = jnp.dot(split_ref[...], chooser_ref[...], preferred_element_type=jnp.float32)
    cells = product[0:count] + product[count : 2 * count] + product[2 * count : 3 * count]
    cells = cells.reshape(dir_count, rows, cols)
    out_ref[0] = cells + total_ref[0] if has_total else cells


def slot_map(uses, slots):
    held = []
    for use, slot in zip(uses, slots):
        held.append(slot if use else (held[-1] if held else None))
    first = next(slot for slot in held if slot is not None)
    held = [first if slot is None else slot for slot in held]

    def index(step):
        place = held[0]
        for k in range(1, len(held)):
            place = place + jnp.where(step >= k, held[k] - held[k - 1], 0)
        return place

    return index


def unpack(halo, chooser, total, after):
    arrays = distinct(halo)
    places = [next(i for i, a in enumerate(arrays) if a is array) for array, _ in halo]
    _, dir_count, rows, cols = arrays[0].shape
    block = (1, dir_count, rows, cols)
    in_specs = []
    for i in range(len(arrays)):
        index = slot_map([place == i for place in places], [slot for _, slot in halo])
        in_specs.append(pl.BlockSpec(block, lambda b, index=index: (index(b), 0, 0, 0)))
    one = pl.BlockSpec(block, lambda b: (b, 0, 0, 0))
    in_specs.append(pl.BlockSpec(chooser.shape, lambda b: (0, 0)))
    extra = [] if total is None else [total]
    in_specs += [one] * len(extra)
    in_specs.append(pl.BlockSpec(memory_space=pl.ANY))
    return pl.pallas_call(
        functools.partial(unpack_kernel, places, len(extra)),
        grid=(len(halo),),
        in_specs=in_specs,
        out_specs=one,
        out_shape=jax.ShapeDtypeStruct((len(halo),) + block[1:], jnp.float32),
        scratch_shapes=[pltpu.VMEM((3 * dir_count * rows, cols), jnp.bfloat16)],
        compiler_params=pltpu.CompilerParams(vmem_limit_bytes=VMEM_BYTES),
        cost_estimate=COST,
        name="unpack",
    )(*arrays, chooser, *extra, after)


def distinct(halo):
    arrays = []
    for array, _ in halo:
        if not any(array is other for other in arrays):
            arrays.append(array)
    return arrays


def source_kernel(dir_count, local_bands, places, *refs):
    meta_ref, tab_ref, land_ref, wind_ref, sum_ref = refs[:5]
    refs = refs[5:]
    out_ref, delta_ref = refs[-2:]
    bands = [(refs[place], slot) for place, slot in places]
    flip = meta_ref[1]

    def density(index, j):
        ref, slot = bands[index + 2]
        return ref[slot, j]

    energy = sum_ref[0] + EPSILON
    first_sum = sum_ref[1]
    mean_sigma = energy / (first_sum + EPSILON)
    ratio = energy / (math.sqrt(GRAVITY) * first_sum + EPSILON)
    mean_k = ratio * ratio
    steepness = energy * mean_k * mean_k / STEEP_REF
    decay = WHITECAP * mean_sigma / mean_k * steepness * steepness
    active = land_ref[...].astype(jnp.float32)
    quad_scale = active * QUAD_COEF / (energy * energy)

    @unrolled(0, dir_count, DELTA_UNROLL)
    def _(j):
        up = lax.rem(j + dir_count + 1 - 4 * flip, dir_count)
        back = lax.rem(j + dir_count - 3 + 4 * flip, dir_count)
        for index in range(-1, local_bands + 1):
            center = density(index, j)
            plus = density(index + 1, up)
            minus = density(index - 1, back)
            delta_ref[index + 1, j] = center * (center * (plus + minus) - 2.0 * (plus * minus))

    growths, keeps, homes = [], [], []
    for index in range(local_bands):
        homes.append(local_band(index, flip, local_bands))
        growth = tab_ref[6 * dir_count + meta_ref[0] * local_bands + homes[index]]
        radian_freq = (2.0 * math.pi * BASE_FREQ) * growth
        wavenum = radian_freq * radian_freq * (1.0 / GRAVITY)
        growths.append(radian_freq)
        keeps.append(active / (1.0 + decay * wavenum))

    @unrolled(0, dir_count, SOURCE_UNROLL)
    def _(j):
        up = lax.rem(j + dir_count + 3 - 4 * flip, dir_count)
        back = lax.rem(j + dir_count - 1 + 4 * flip, dir_count)
        wind = tab_ref[4 * dir_count + j] * wind_ref[0] + tab_ref[5 * dir_count + j] * wind_ref[1]
        for index in range(local_bands):
            radian_freq = growths[index]
            quad = delta_ref[index, back] + delta_ref[index + 2, up] - 2.0 * delta_ref[index + 1, j]
            rate = WIND_COEF * radian_freq
            gain = jnp.maximum((rate * radian_freq) * wind + (1.0 - rate), 1.0)
            out_ref[homes[index], j] = density(index, j) * gain * keeps[index] + quad * quad_scale


def source(strip, shape, meta, table, land_sea, wind, sums, sum_block, bands, previous):
    local_bands, dir_count, row_count, cols = shape
    lanes = SOURCE_LANES if cols % SOURCE_LANES == 0 else cols
    arrays = distinct(bands)
    places = [(next(i for i, a in enumerate(arrays) if a is array), slot) for array, slot in bands]
    smem = pl.BlockSpec(memory_space=pltpu.SMEM)
    part = lambda ref: pl.BlockSpec((ref.shape[0], dir_count, STRIP, lanes), lambda c: (0, 0, 0, c))
    in_specs = [smem, smem]
    in_specs.append(pl.BlockSpec((STRIP, lanes), lambda c: (strip, c)))
    in_specs.append(pl.BlockSpec((2, STRIP, lanes), lambda c: (0, strip, c)))
    in_specs.append(pl.BlockSpec((2, STRIP, lanes), lambda c: (0, sum_block, c)))
    in_specs += [part(ref) for ref in arrays]
    operands = [meta, table, land_sea, wind, sums, *arrays]
    aliases = {}
    if previous is not None:
        in_specs.append(pl.BlockSpec(memory_space=pl.ANY))
        aliases = {len(operands): 0}
        operands.append(previous)
    return pl.pallas_call(
        functools.partial(source_kernel, dir_count, local_bands, places),
        grid=(cols // lanes,),
        in_specs=in_specs,
        out_specs=pl.BlockSpec((local_bands, dir_count, STRIP, lanes), lambda c: (0, 0, strip, c)),
        out_shape=jax.ShapeDtypeStruct(shape, jnp.float32),
        scratch_shapes=[pltpu.VMEM((local_bands + 2, dir_count, STRIP, lanes), jnp.float32)],
        input_output_aliases=aliases,
        compiler_params=pltpu.CompilerParams(vmem_limit_bytes=VMEM_BYTES),
        cost_estimate=COST,
        name="source",
    )(*operands)


def spec_total(value):
    count = lax.axis_size("spec")
    if count & (count - 1):
        return lax.psum(value, "spec")
    if count == 8:
        value = value + lax.ppermute(value, "spec", [(i, i ^ 1) for i in range(count)])
        others = [lax.ppermute(value, "spec", [(i, i ^ k) for i in range(count)]) for k in (2, 4, 6)]
        return (value + others[0]) + (others[1] + others[2])
    reach = 1
    while reach < count:
        value = value + lax.ppermute(value, "spec", [(i, i ^ reach) for i in range(count)])
        reach *= 2
    return value


def relay_pairs(count, first_across):
    first, second = [], []
    for low in range(1, count - 1, 2):
        for source, goal in ((low + 1, low), (low, low + 1)):
            rank = low if source > goal else count - 2 - low
            if first_across(rank):
                first.append((source, source ^ 1))
                second.append((source ^ 1, goal))
            else:
                first.append((source, goal))
                second.append((goal, goal))
    return first, second


def along_pairs(count):
    first, second = [], []
    for low in range(1, count - 1, 2):
        for source, goal in ((low + 1, low), (low, low + 1)):
            first.append((source, goal ^ 1))
            second.append((goal ^ 1, goal))
    return first, second


def hold(value, *others):
    whole = pl.BlockSpec(memory_space=pl.ANY)
    return pl.pallas_call(
        lambda *refs: None,
        in_specs=[whole] * (1 + len(others)),
        out_specs=whole,
        out_shape=jax.ShapeDtypeStruct(value.shape, value.dtype),
        input_output_aliases={0: 0},
        cost_estimate=COST,
        name="hold",
    )(value, *others)


def shards(spectrum, land_sea, sea_index, sea_count, wind_speed, wind_dir, slope_x, slope_y):
    local_bands, dir_count, row_count, cols = spectrum.shape
    spec_count = lax.axis_size("spec")
    geo_count = lax.axis_size("geo")
    pos = lax.axis_index("spec").astype(jnp.int32)
    table = jnp.asarray(tables(local_bands * spec_count, dir_count))
    inner, outer, spill = (1, 2), (0, 3), 2
    kept = (1, 0, 3)
    size = min(2, local_bands)
    groups = list(range(0, local_bands, size))
    paired = local_bands == 4 and spec_count % 2 == 0
    meta = jnp.stack([pos, pos % 2 if paired else 0 * pos])
    choose = plan(land_sea, kept, spill, (0,), False)

    args = (meta, table, spectrum, land_sea, slope_x, slope_y)
    bands = {s: [] for s in range(4)}
    sends = {s: [] for s in kept}
    rims, prior = [], []
    for group in groups:
        strip_a, strip_b, send, sums, head, tail = propagate(
            inner, 1, (0,), (False,), False, group, size, *args, prior, (), choose[:1]
        )
        bands[1].append(strip_a)
        bands[2].append(strip_b)
        sends[1].append([send])
        rims.append((head, tail))
        prior = [sums]
    choose = list(choose) + list(plan(land_sea, kept, spill, (1, 2), False))
    ups = [(i, i + 1) for i in range(geo_count - 1)]
    downs = [(i + 1, i) for i in range(geo_count - 1)]
    for index, group in enumerate(groups):
        head, tail = rims[index]
        lower = lax.ppermute(tail, "geo", ups)
        upper = lax.ppermute(head, "geo", downs)
        split = paired and index == 0
        strip_a, strip_b, *send, sums = propagate(
            outer, None, (0, 1), (split, False), True, group, size, *args, prior, (lower, upper, bands[2][index]), choose[1:]
        )
        bands[0].append(strip_a)
        bands[3].append(strip_b)
        sends[0].append(send[:-1])
        sends[3].append(send[-1:])
        prior = [sums]
    sums = prior[0]
    scale = (28.0 * USTAR_RATIO / GRAVITY) * wind_speed
    wind = jnp.stack([scale * jnp.cos(wind_dir), scale * jnp.sin(wind_dir)])
    back = dict(zip(kept, plan(land_sea, kept, spill, (0, 1, 2), True)))

    def finish(s, halo, result, total):
        if s != spill:
            total = unpack(halo, back[s], total, sums if result is None else result)
        own = [(array, i) for array in bands[s] for i in range(size)]
        members = halo[:2] + own + halo[2:]
        result = source(s, spectrum.shape, meta, table, land_sea, wind, sums, s, members, result)
        return result, total

    result = total = None
    if paired:
        partner = [(i, i ^ 1) for i in range(spec_count)]
        across = relay_pairs(spec_count, lambda rank: True)
        most = relay_pairs(spec_count, lambda rank: 2 * rank >= spec_count - 2)
        some = relay_pairs(spec_count, lambda rank: rank >= spec_count - 3)
        along = along_pairs(spec_count)

        def send(value, pairs):
            return lax.ppermute(value, "spec", pairs)

        def members(far, near):
            return [(far[-1], far[-1].shape[0] - 1), (far[0], 0), (near, 1), (near, 0)]

        far_1 = send(sends[1][0][0], across[0])
        near_1 = send(sends[1][1][0], partner)
        sums = spec_total(hold(sums, near_1))
        near_0 = send(hold(sends[0][1][0], far_1), partner)
        far_3 = send(sends[3][0][0], along[0])
        far_0 = [send(value, pairs[0]) for value, pairs in zip(sends[0][0], (some, most))]
        far_1 = send(far_1, across[1])
        far_3 = send(far_3, along[1])
        far_0 = [send(value, pairs[1]) for value, pairs in zip(far_0, (some, most))]
        near_3 = send(hold(sends[3][1][0], near_0), partner)
        result, total = finish(1, members([far_1], near_1), result, total)
        result, total = finish(0, members(far_0, near_0), result, total)
        result, total = finish(3, members([far_3], near_3), result, total)
    else:

        def hop(value, count):
            pairs = [(i, i + count) for i in range(spec_count) if 0 <= i + count < spec_count]
            return lax.ppermute(value, "spec", pairs)

        sums = spec_total(sums)
        for s in kept:
            first, last = sends[s][0][0], sends[s][-1][0]
            if size == 2:
                lower, upper = hop(last, 1), hop(first, -1)
                halo = [(lower, 0), (lower, 1), (upper, 0), (upper, 1)]
            else:
                halo = [(hop(last, 2), 0), (hop(last, 1), 0), (hop(first, -1), 0), (hop(first, -2), 0)]
            result, total = finish(s, halo, result, total)
    return finish(spill, [(total, i) for i in range(4)], result, total)[0]


def solution(mesh):
    placed = (
        P("spec", None, "geo", None),
        P("geo", None),
        P("geo", None),
        P("geo"),
        P("geo", None),
        P("geo", None),
        P("geo", None),
        P("geo", None),
    )
    return jax.shard_map(
        shards, mesh=mesh, in_specs=placed, out_specs=P("spec", None, "geo", None), check_vma=False
    )
```

```python
import functools
import math

import jax
import jax.numpy as jnp
import numpy as np
from jax import lax
from jax.experimental import pallas as pl
from jax.experimental.pallas import tpu as pltpu
from jax.sharding import PartitionSpec as P

GRAVITY = 9.81
BASE_FREQ = 0.035
GROWTH = 1.1
COURANT_TOP = 0.9
TURN_TOP = 1.2
SPACING = 0.1
USTAR_RATIO = 0.035
WIND_COEF = 0.0375
WHITECAP = 0.36
STEEP_REF = 1.6
EPSILON = 1e-06
QUAD_COEF = 100.0

STRIP = 8
LANES = 128
VMEM_BYTES = 56 * 1024 * 1024
ROW_UNROLL = 9
TURN_UNROLL = 3
DELTA_UNROLL = 4
SOURCE_UNROLL = 4
SOURCE_LANES = 256
SPARE = 4
COST = pl.CostEstimate(flops=1024, bytes_accessed=1024, transcendentals=0)


def tables(band_total, dir_count):
    dtheta = 2.0 * math.pi / dir_count
    angles = (np.arange(dir_count) + 0.5) * dtheta
    faces = np.arange(dir_count) * dtheta
    parts = [
        np.abs(np.cos(angles)),
        np.abs(np.sin(angles)),
        np.sin(faces),
        np.cos(faces),
        np.cos(angles),
        np.sin(angles),
        GROWTH ** np.arange(band_total),
    ]
    return np.concatenate(parts).astype(np.float32)


def sign_runs(dir_count):
    angles = (np.arange(dir_count) + 0.5) * 2.0 * math.pi / dir_count
    signs = [(bool(np.cos(a) >= 0), bool(np.sin(a) >= 0)) for a in angles]
    runs, first = [], 0
    for j in range(1, dir_count + 1):
        if j == dir_count or signs[j] != signs[first]:
            runs.append((first, j) + signs[first])
            first = j
    return runs


def unrolled(first, last, count):
    def wrap(body):
        turns = (last - first) // count
        if turns:

            @pl.loop(0, turns)
            def _(turn):
                for k in range(count):
                    body(first + turn * count + k)

        for j in range(first + turns * count, last):
            body(j)

    return wrap


def plan_kernel(kept, spill, wanted, back, land_ref, *out_refs):
    cols = land_ref.shape[1]
    flags = [land_ref[STRIP * s : STRIP * s + 1, :].astype(jnp.float32) for s in (spill,) + tuple(kept)]
    rows = [flags[0]] + [1.0 - flag for flag in flags[1:]]
    rows += [jnp.zeros((1, cols), jnp.float32)] * (8 - len(rows))
    table = jnp.concatenate(rows, axis=0)
    first = lax.broadcasted_iota(jnp.int32, (cols, cols), 0)
    second = lax.broadcasted_iota(jnp.int32, (cols, cols), 1)
    block = STRIP
    starts = lax.broadcasted_iota(jnp.int32, (8, cols), 1) % block == 0
    narrow = jnp.where(starts, table, 0.0).astype(jnp.bfloat16)
    before = jnp.where(first < (second & ~(block - 1)), 1.0, 0.0).astype(jnp.bfloat16)
    ranks = jnp.dot(narrow, before, preferred_element_type=jnp.float32)
    phase = (first & (block - 1)) == (second & (block - 1))
    marks = [jnp.where(table[0:1] > 0.5, ranks[0:1], -1.0)]
    offset = jnp.zeros((1, 1), jnp.float32)
    for index in range(len(kept)):
        hole = table[index + 1 : index + 2, :]
        marks.append(jnp.where(hole > 0.5, ranks[index + 1 : index + 2, :] + offset, -2.0))
        offset = offset + jnp.sum(hole, axis=1, keepdims=True) * (1.0 / block)
    marks = jnp.concatenate(marks + [jnp.zeros((1, cols), jnp.float32)] * (8 - len(marks)), axis=0)
    columns = marks.T
    for index, out_ref in zip(wanted, out_refs):
        if back:
            match = jnp.abs(columns[:, index + 1 : index + 2] - marks[0:1, :]) < 0.5
        else:
            match = jnp.abs(columns[:, 0:1] - marks[index + 1 : index + 2, :]) < 0.5
        out_ref[...] = jnp.where(jnp.logical_and(phase, match), 1.0, 0.0).astype(jnp.bfloat16)


def plan(land_sea, kept, spill, wanted, back):
    cols = land_sea.shape[1]
    return pl.pallas_call(
        functools.partial(plan_kernel, kept, spill, wanted, back),
        out_shape=[jax.ShapeDtypeStruct((cols, cols), jnp.bfloat16)] * len(wanted),
        compiler_params=pltpu.CompilerParams(vmem_limit_bytes=VMEM_BYTES),
        name="plan_back" if back else "plan",
    )(land_sea)


def taps(courant):
    rest = (1.0 - courant * courant) * (1.0 / 6.0)
    down = courant * (0.5 - 0.5 * courant - rest)
    centre = courant * (0.5 + 0.5 * courant + 2.0 * rest)
    far = -courant * rest
    return -down, 1.0 - centre + down, centre - far, far


def lane_shift(pieces, shift, lane_ids):
    rolled = [pltpu.roll(piece, shift % LANES, 1) for piece in pieces]
    zero = jnp.zeros_like(pieces[0])
    moved = []
    for index in range(len(pieces)):
        if shift > 0:
            other = rolled[index - 1] if index > 0 else zero
            moved.append(jnp.where(lane_ids < shift, other, rolled[index]))
        else:
            other = rolled[index + 1] if index + 1 < len(pieces) else zero
            moved.append(jnp.where(lane_ids >= LANES + shift, other, rolled[index]))
    return moved


def split_store(cells, split_ref):
    count = cells.shape[0]
    high = cells.astype(jnp.bfloat16)
    rest = cells - high.astype(jnp.float32)
    mid = rest.astype(jnp.bfloat16)
    split_ref[0:count, :] = high
    split_ref[count : 2 * count, :] = mid


def local_band(index, flip, local_bands):
    return index + flip * (local_bands - 1 - 2 * index)


def take(refs, count):
    return refs[:count], refs[count:]


def propagate_kernel(strips, dests, sends, spills, edge, chained, rims, group, size, dir_count, local_bands, *refs):
    (meta_ref, tab_ref, spec_ref, land_ref, sx_ref, sy_ref), refs = take(list(refs), 6)
    prior_refs, refs = take(refs, chained)
    rim_refs, refs = take(refs, 2 if edge or rims else 0)
    spill_refs, refs = take(refs, len(spills))
    choosers, refs = take(refs, len(dests))
    out_refs, refs = take(refs, len(strips))
    send_refs, refs = take(refs, len(sends))
    (sum_ref,), refs = take(refs, 1)
    edge_refs, refs = take(refs, 0 if edge else 2)
    turn_ref, moved_ref, split_ref, wet_ref = refs

    row_count, cols = land_ref.shape
    strip_count = row_count // STRIP
    step = pl.program_id(0)
    band = meta_ref[0] * local_bands + local_band(group + step, meta_ref[1], local_bands)
    growth = tab_ref[6 * dir_count + band]
    courant = COURANT_TOP / growth
    turn_rate = TURN_TOP / growth
    radian_freq = (2.0 * math.pi * BASE_FREQ) * growth
    weight = SPACING * radian_freq * (2.0 * math.pi / dir_count)
    row_ids = lax.broadcasted_iota(jnp.int32, (STRIP, cols), 0)
    lane_ids = lax.broadcasted_iota(jnp.int32, (STRIP, LANES), 1)

    @pl.when(step == 0)
    def _():
        sum_ref[...] = prior_refs[0][...] if chained else jnp.zeros_like(sum_ref)
        wet_ref[...] = land_ref[...].astype(jnp.float32)
        if rims:
            for edge_ref, rim_ref in zip(edge_refs, rim_refs):
                edge_ref[...] = rim_ref[...]

        @pl.loop(0, dir_count)
        def _(f):
            face_sin = tab_ref[2 * dir_count + f]
            face_cos = tab_ref[3 * dir_count + f]
            for slot, s in enumerate(strips):
                rows = slice(STRIP * s, STRIP * (s + 1))
                turn_ref[slot, f] = face_sin * sx_ref[rows, :] - face_cos * sy_ref[rows, :]

    for first, last, cos_up, sin_up in sign_runs(dir_count):

        @unrolled(first, last, ROW_UNROLL)
        def _(j):
            row_taps = taps(courant * tab_ref[j])
            col_taps = taps(courant * tab_ref[dir_count + j])
            known = {}

            def wet(s):
                return wet_ref[STRIP * s : STRIP * (s + 1), :]

            def cells(s):
                if s not in known:
                    if s < 0:
                        blank = jnp.zeros((STRIP - 2, cols), jnp.float32)
                        known[s] = jnp.concatenate([blank, rim_refs[0][0, j]], axis=0)
                    elif s == strip_count:
                        blank = jnp.zeros((STRIP - 2, cols), jnp.float32)
                        known[s] = jnp.concatenate([rim_refs[1][0, j], blank], axis=0)
                    else:
                        known[s] = spec_ref[0, j, STRIP * s : STRIP * (s + 1), :] * wet(s)
                return known[s]

            def rolled(s, shift):
                if (s, shift) not in known:
                    known[s, shift] = pltpu.roll(cells(s), shift % STRIP, 0)
                return known[s, shift]

            def row_shift(s, shift):
                other = rolled(s - 1 if shift > 0 else s + 1, shift)
                outside = row_ids < shift if shift > 0 else row_ids >= STRIP + shift
                return jnp.where(outside, other, rolled(s, shift))

            if not edge:
                edge_refs[0][group + step, j] = cells(0)[0:2]
                edge_refs[1][group + step, j] = cells(strip_count - 1)[STRIP - 2 :]
            for slot, s in enumerate(strips):
                wet_s = wet(s)
                way = 1 if cos_up else -1
                moved = (
                    row_taps[1] * cells(s)
                    + row_taps[0] * row_shift(s, -way)
                    + row_taps[2] * row_shift(s, way)
                    + row_taps[3] * row_shift(s, 2 * way)
                ) * wet_s
                way = 1 if sin_up else -1
                pieces = [moved[:, LANES * c : LANES * (c + 1)] for c in range(cols // LANES)]
                down = lane_shift(pieces, -way, lane_ids)
                upwind = lane_shift(pieces, way, lane_ids)
                far = lane_shift(pieces, 2 * way, lane_ids)
                for c in range(cols // LANES):
                    lanes = slice(LANES * c, LANES * (c + 1))
                    moved_ref[slot, j + 2, :, lanes] = (
                        col_taps[1] * pieces[c]
                        + col_taps[0] * down[c]
                        + col_taps[2] * upwind[c]
                        + col_taps[3] * far[c]
                    ) * wet_s[:, lanes]

    moved_ref[:, 0:2] = moved_ref[:, dir_count : dir_count + 2]
    moved_ref[:, dir_count + 2 : dir_count + 4] = moved_ref[:, 2:4]

    def face_flux(slot, f, turning):
        far_left, left = moved_ref[slot, f], moved_ref[slot, f + 1]
        right, far_right = moved_ref[slot, f + 2], moved_ref[slot, f + 3]
        rate = turn_rate * turning
        square = rate * rate
        slope = right - left
        bend = jnp.where(rate >= 0, slope - (left - far_left), (far_right - right) - slope)
        return rate * (
            0.5 * ((left + right) - rate * slope) - (1.0 / 6.0 - square * (1.0 / 6.0)) * bend
        )

    def turn(step, carry):
        carry = list(carry)
        for k in range(TURN_UNROLL):
            f = step * TURN_UNROLL + k + 1
            face = f if k < TURN_UNROLL - 1 else lax.rem(f, dir_count)
            for slot in range(len(strips)):
                lower, total = carry[slot]
                flux = face_flux(slot, f, turn_ref[slot, face])
                cell = jnp.maximum(moved_ref[slot, f + 1] - (flux - lower), 0.0)
                out_refs[slot][0, f - 1] = cell
                carry[slot] = (flux, total + cell)
        return tuple(carry)

    zero = jnp.zeros((STRIP, cols), jnp.float32)
    start = tuple((face_flux(slot, 0, turn_ref[slot, 0]), zero) for slot in range(len(strips)))
    ends = lax.fori_loop(0, dir_count // TURN_UNROLL, turn, start)
    for slot, (_, total) in enumerate(ends):
        rows = slice(STRIP * strips[slot], STRIP * (strips[slot] + 1))
        sum_ref[0, rows, :] += weight * total
        sum_ref[1, rows, :] += (SPACING * 2.0 * math.pi / dir_count) * total

    count = dir_count * STRIP
    if spills:
        for (low, high), spill_ref in zip(spills, spill_refs):

            @pl.when(jnp.logical_and(step >= low, step < high))
            def _():
                split_store(spill_ref[0].reshape(count, cols), split_ref)

    else:
        split_store(out_refs[-1][0].reshape(count, cols), split_ref)
    filled = []
    for chooser, dest in zip(choosers, dests):
        product = jnp.dot(split_ref[...], chooser[...], preferred_element_type=jnp.float32)
        product = product[0:count] + product[count : 2 * count]
        filled.append(out_refs[dest][0] + product.reshape(dir_count, STRIP, cols))
    for (places, low, length, _), send_ref in zip(sends, send_refs):

        @pl.when(jnp.logical_and(step >= low, step < low + length))
        def _():
            for index, place in enumerate(places):
                start = (index * length + step - low) * dir_count
                send_ref[pl.ds(start, dir_count)] = filled[place]


def propagate(strips, dests, sends, edge, group, size, meta, table, spectrum, land_sea, slope_x, slope_y, prior, rims, spills, choosers):
    local_bands, dir_count, row_count, cols = spectrum.shape
    whole = lambda shape: pl.BlockSpec(shape, lambda b, meta: (0,) * len(shape))
    clip = lambda b, low, length: jnp.clip(b - low, 0, length - 1)
    flat = whole((row_count, cols))
    in_specs = [pl.BlockSpec(memory_space=pltpu.SMEM)]
    in_specs += [
        pl.BlockSpec(
            (1, dir_count, row_count, cols),
            lambda b, meta: (local_band(b + group, meta[1], local_bands), 0, 0, 0),
        )
    ]
    in_specs += [flat, flat, flat]
    sums = (2, row_count, cols)
    in_specs += [whole(sums)] * len(prior)
    if edge:
        in_specs += [pl.BlockSpec((1, dir_count, 2, cols), lambda b, meta: (b, 0, 0, 0))] * 2
    else:
        in_specs += [whole(rim.shape) for rim in rims]
    for _, low, high in spills:
        in_specs.append(
            pl.BlockSpec(
                (1, dir_count, STRIP, cols), lambda b, meta, low=low, high=high: (clip(b, low, high - low), 0, 0, 0)
            )
        )
    in_specs += [whole((cols, cols))] * len(choosers)
    shape = lambda *dims: jax.ShapeDtypeStruct(dims, jnp.float32)
    out_shape = [shape(size, dir_count, STRIP, cols)] * len(strips)
    out_specs = [pl.BlockSpec((1, dir_count, STRIP, cols), lambda b, meta: (b, 0, 0, 0))] * len(strips)
    for places, low, length, room in sends:
        block = (len(places) * length * dir_count + room, STRIP, cols)
        out_shape.append(shape(*block))
        out_specs.append(whole(block))
    out_shape.append(shape(*sums))
    out_specs.append(whole(sums))
    if not edge:
        out_shape += [shape(local_bands, dir_count, 2, cols)] * 2
        out_specs += [whole((local_bands, dir_count, 2, cols))] * 2
    return pl.pallas_call(
        functools.partial(
            propagate_kernel,
            strips,
            dests,
            sends,
            [(low, high) for _, low, high in spills],
            edge,
            len(prior),
            not edge and len(rims) > 0,
            group,
            size,
            dir_count,
            local_bands,
        ),
        grid_spec=pltpu.PrefetchScalarGridSpec(
            num_scalar_prefetch=1,
            grid=(size,),
            in_specs=in_specs,
            out_specs=out_specs,
            scratch_shapes=[
                pltpu.VMEM((len(strips), dir_count, STRIP, cols), jnp.float32),
                pltpu.VMEM((len(strips), dir_count + 4, STRIP, cols), jnp.float32),
                pltpu.VMEM((2 * dir_count * STRIP, cols), jnp.bfloat16),
                pltpu.VMEM((row_count, cols), jnp.float32),
            ],
        ),
        out_shape=out_shape,
        compiler_params=pltpu.CompilerParams(vmem_limit_bytes=VMEM_BYTES),
        cost_estimate=COST,
        name="propagate_edge" if edge else "propagate_inner",
    )(meta, table, spectrum, land_sea, slope_x, slope_y, *prior, *rims, *[spill[0] for spill in spills], *choosers)


def unpack_kernel(places, has_total, *refs):
    out_ref, split_ref = refs[-2:]
    total_ref, chooser_ref = refs[-4], refs[-4 - has_total]
    _, dir_count, rows, cols = out_ref.shape
    count = dir_count * rows
    for slot, place in enumerate(places):

        @pl.when(pl.program_id(0) == slot)
        def _():
            split_store(refs[place][...].reshape(count, cols), split_ref)

    product = jnp.dot(split_ref[...], chooser_ref[...], preferred_element_type=jnp.float32)
    cells = product[0:count] + product[count : 2 * count]
    cells = cells.reshape(dir_count, rows, cols)
    out_ref[0] = cells + total_ref[0] if has_total else cells


def slot_map(uses, slots):
    held = []
    for use, slot in zip(uses, slots):
        held.append(slot if use else (held[-1] if held else None))
    first = next(slot for slot in held if slot is not None)
    held = [first if slot is None else slot for slot in held]

    def index(step):
        place = held[0]
        for k in range(1, len(held)):
            place = place + jnp.where(step >= k, held[k] - held[k - 1], 0)
        return place

    return index


def flat_bands(array):
    return array.reshape((-1,) + array.shape[-2:])


def unpack(halo, dir_count, chooser, total, after):
    arrays = distinct(halo)
    places = [next(i for i, a in enumerate(arrays) if a is array) for array, _ in halo]
    rows, cols = arrays[0].shape[-2:]
    block = (1, dir_count, rows, cols)
    in_specs = []
    for i in range(len(arrays)):
        index = slot_map([place == i for place in places], [slot for _, slot in halo])
        in_specs.append(pl.BlockSpec(block[1:], lambda b, index=index: (index(b), 0, 0)))
    one = pl.BlockSpec(block, lambda b: (b, 0, 0, 0))
    in_specs.append(pl.BlockSpec(chooser.shape, lambda b: (0, 0)))
    extra = [] if total is None else [total]
    in_specs += [one] * len(extra)
    in_specs.append(pl.BlockSpec(memory_space=pl.ANY))
    return pl.pallas_call(
        functools.partial(unpack_kernel, places, len(extra)),
        grid=(len(halo),),
        in_specs=in_specs,
        out_specs=one,
        out_shape=jax.ShapeDtypeStruct((len(halo),) + block[1:], jnp.float32),
        scratch_shapes=[pltpu.VMEM((2 * dir_count * rows, cols), jnp.bfloat16)],
        compiler_params=pltpu.CompilerParams(vmem_limit_bytes=VMEM_BYTES),
        cost_estimate=COST,
        name="unpack",
    )(*[flat_bands(array) for array in arrays], chooser, *extra, after)


def distinct(halo):
    arrays = []
    for array, _ in halo:
        if not any(array is other for other in arrays):
            arrays.append(array)
    return arrays


def source_kernel(dir_count, local_bands, places, *refs):
    bands = [(refs[5 + place], slot) for place, slot in places]

    def density(index, j):
        ref, slot = bands[index + 2]
        return ref[slot * dir_count + j]

    source_body(dir_count, local_bands, density, *refs[:5], *refs[-2:])


def source_body(dir_count, local_bands, density, meta_ref, tab_ref, land_ref, wind_ref, sum_ref, out_ref, delta_ref):
    flip = meta_ref[1]
    energy = sum_ref[0] + EPSILON
    first_sum = sum_ref[1]
    mean_sigma = energy / (first_sum + EPSILON)
    ratio = energy / (math.sqrt(GRAVITY) * first_sum + EPSILON)
    mean_k = ratio * ratio
    steepness = energy * mean_k * mean_k / STEEP_REF
    decay = WHITECAP * mean_sigma / mean_k * steepness * steepness
    active = land_ref[...].astype(jnp.float32)
    quad_scale = active * QUAD_COEF / (energy * energy)

    @unrolled(0, dir_count, DELTA_UNROLL)
    def _(j):
        up = lax.rem(j + dir_count + 1 - 4 * flip, dir_count)
        back = lax.rem(j + dir_count - 3 + 4 * flip, dir_count)
        for index in range(-1, local_bands + 1):
            center = density(index, j)
            plus = density(index + 1, up)
            minus = density(index - 1, back)
            delta_ref[index + 1, j] = center * (center * (plus + minus) - 2.0 * (plus * minus))

    growths, keeps, homes = [], [], []
    for index in range(local_bands):
        homes.append(local_band(index, flip, local_bands))
        growth = tab_ref[6 * dir_count + meta_ref[0] * local_bands + homes[index]]
        radian_freq = (2.0 * math.pi * BASE_FREQ) * growth
        wavenum = radian_freq * radian_freq * (1.0 / GRAVITY)
        growths.append(radian_freq)
        keeps.append(active / (1.0 + decay * wavenum))

    @unrolled(0, dir_count, SOURCE_UNROLL)
    def _(j):
        up = lax.rem(j + dir_count + 3 - 4 * flip, dir_count)
        back = lax.rem(j + dir_count - 1 + 4 * flip, dir_count)
        wind = tab_ref[4 * dir_count + j] * wind_ref[0] + tab_ref[5 * dir_count + j] * wind_ref[1]
        for index in range(local_bands):
            radian_freq = growths[index]
            quad = delta_ref[index, back] + delta_ref[index + 2, up] - 2.0 * delta_ref[index + 1, j]
            rate = WIND_COEF * radian_freq
            gain = jnp.maximum((rate * radian_freq) * wind + (1.0 - rate), 1.0)
            out_ref[homes[index], j] = density(index, j) * gain * keeps[index] + quad * quad_scale


def spans_of(bands):
    arrays = distinct(bands)
    spans = []
    for array in arrays:
        slots = [slot for other, slot in bands if other is array]
        low, count = min(slots), max(slots) - min(slots) + 1
        spans.append((low // count, count) if low % count == 0 else (0, max(slots) + 1))
    places = []
    for array, slot in bands:
        index = next(i for i, a in enumerate(arrays) if a is array)
        places.append((index, slot - spans[index][0] * spans[index][1]))
    return arrays, spans, places


def last_kernel(dir_count, local_bands, halves, unpack_places, band_places, counts, *refs):
    scalar, refs = take(list(refs), 5)
    halo_refs = []
    for count in counts[0]:
        found, refs = take(refs, count)
        halo_refs.append(found)
    (prior_ref, *choosers), refs = take(refs, 1 + len(unpack_places))
    band_refs = []
    for count in counts[1]:
        found, refs = take(refs, count)
        band_refs.append(found)
    _, out_ref, delta_ref, split_ref, total_ref = refs
    step = pl.program_id(0)
    halo_count = len(unpack_places[0])
    _, rows, cols = halo_refs[0][0].shape
    lanes = out_ref.shape[-1]
    count = dir_count * rows

    @pl.when(step < halo_count)
    def _():
        total = prior_ref[...]
        for found, places, chooser in zip(halo_refs, unpack_places, choosers):
            for slot, place in enumerate(places):

                @pl.when(step == slot)
                def _():
                    split_store(found[place][...].reshape(count, cols), split_ref)

            product = jnp.dot(split_ref[...], chooser[...], preferred_element_type=jnp.float32)
            total = total + (product[0:count] + product[count : 2 * count]).reshape(dir_count, rows, cols)
        for half in range(halves):
            total_ref[half, pl.ds(step * dir_count, dir_count)] = total[:, :, half * lanes : (half + 1) * lanes]

    half = lax.rem(jnp.maximum(step - halo_count, 0), halves)
    for turn, (found, places) in enumerate(zip(band_refs, band_places)):
        first = halo_count + turn * halves

        @pl.when(jnp.logical_and(step >= first, step < first + halves))
        def _():
            def density(index, j):
                place, slot = places[index + 2]
                if place is None:
                    return total_ref[half, slot * dir_count + j]
                return found[place][slot * dir_count + j]

            source_body(dir_count, local_bands, density, *scalar, out_ref, delta_ref)


def last_sources(strips, shape, meta, table, land_sea, wind, sums, halos, members, choosers, total, previous):
    local_bands, dir_count, row_count, cols = shape
    lanes = SOURCE_LANES if cols % SOURCE_LANES == 0 else cols
    halves = cols // lanes
    halo_count = len(halos[0])
    smem = pl.BlockSpec(memory_space=pltpu.SMEM)

    def turn(t):
        return jnp.maximum(t - halo_count, 0) // halves

    def strip(t):
        place = strips[0]
        for k in range(1, len(strips)):
            place = place + jnp.where(turn(t) >= k, strips[k] - strips[k - 1], 0)
        return place

    def half(t):
        return lax.rem(jnp.maximum(t - halo_count, 0), halves)

    def part(t, k):
        return jnp.clip(t - halo_count - k * halves, 0, halves - 1)

    in_specs = [smem, smem]
    in_specs.append(pl.BlockSpec((STRIP, lanes), lambda t: (strip(t), half(t))))
    in_specs += [pl.BlockSpec((2, STRIP, lanes), lambda t: (0, strip(t), half(t)))] * 2
    operands = [meta, table, land_sea, wind, sums]
    block = (dir_count, STRIP, cols)
    unpack_places, counts = [], ([], [])
    for halo in halos:
        arrays = distinct(halo)
        places = [next(i for i, a in enumerate(arrays) if a is array) for array, _ in halo]
        for i, array in enumerate(arrays):
            index = slot_map([place == i for place in places], [slot for _, slot in halo])
            in_specs.append(pl.BlockSpec(block, lambda t, index=index: (index(t), 0, 0)))
            operands.append(flat_bands(array))
        unpack_places.append(places)
        counts[0].append(len(arrays))
    in_specs.append(pl.BlockSpec(block, lambda t: (jnp.minimum(t, halo_count - 1), 0, 0)))
    operands.append(flat_bands(total))
    in_specs += [pl.BlockSpec((cols, cols), lambda t: (0, 0))] * len(choosers)
    operands += choosers
    band_places = []
    for k in range(len(strips)):
        arrays, spans, found = spans_of([entry for entry in members[k] if entry[0] is not None])
        found = iter(found)
        places = [(None, slot) if array is None else next(found) for array, slot in members[k]]
        for array, (first, count) in zip(arrays, spans):
            in_specs.append(
                pl.BlockSpec(
                    (count * dir_count, STRIP, lanes), lambda t, first=first, k=k: (first, 0, part(t, k))
                )
            )
            operands.append(flat_bands(array))
        band_places.append(places)
        counts[1].append(len(arrays))
    in_specs.append(pl.BlockSpec(memory_space=pl.ANY))
    operands.append(previous)
    return pl.pallas_call(
        functools.partial(last_kernel, dir_count, local_bands, halves, unpack_places, band_places, counts),
        grid=(halo_count + len(strips) * halves,),
        in_specs=in_specs,
        out_specs=pl.BlockSpec((local_bands, dir_count, STRIP, lanes), lambda t: (0, 0, strip(t), half(t))),
        out_shape=jax.ShapeDtypeStruct(shape, jnp.float32),
        scratch_shapes=[
            pltpu.VMEM((local_bands + 2, dir_count, STRIP, lanes), jnp.float32),
            pltpu.VMEM((2 * dir_count * STRIP, cols), jnp.bfloat16),
            pltpu.VMEM((halves, halo_count * dir_count, STRIP, lanes), jnp.float32),
        ],
        input_output_aliases={len(operands) - 1: 0},
        compiler_params=pltpu.CompilerParams(vmem_limit_bytes=VMEM_BYTES),
        cost_estimate=COST,
        name="last_sources",
    )(*operands)


def source(strip, shape, meta, table, land_sea, wind, sums, sum_block, bands, previous):
    local_bands, dir_count, row_count, cols = shape
    lanes = SOURCE_LANES if cols % SOURCE_LANES == 0 else cols
    arrays, spans, places = spans_of(bands)
    smem = pl.BlockSpec(memory_space=pltpu.SMEM)
    part = lambda first, count: pl.BlockSpec((count * dir_count, STRIP, lanes), lambda c: (first, 0, c))
    in_specs = [smem, smem]
    in_specs.append(pl.BlockSpec((STRIP, lanes), lambda c: (strip, c)))
    in_specs.append(pl.BlockSpec((2, STRIP, lanes), lambda c: (0, strip, c)))
    in_specs.append(pl.BlockSpec((2, STRIP, lanes), lambda c: (0, sum_block, c)))
    in_specs += [part(*span) for span in spans]
    operands = [meta, table, land_sea, wind, sums, *[flat_bands(array) for array in arrays]]
    aliases = {}
    if previous is not None:
        in_specs.append(pl.BlockSpec(memory_space=pl.ANY))
        aliases = {len(operands): 0}
        operands.append(previous)
    return pl.pallas_call(
        functools.partial(source_kernel, dir_count, local_bands, places),
        grid=(cols // lanes,),
        in_specs=in_specs,
        out_specs=pl.BlockSpec((local_bands, dir_count, STRIP, lanes), lambda c: (0, 0, strip, c)),
        out_shape=jax.ShapeDtypeStruct(shape, jnp.float32),
        scratch_shapes=[pltpu.VMEM((local_bands + 2, dir_count, STRIP, lanes), jnp.float32)],
        input_output_aliases=aliases,
        compiler_params=pltpu.CompilerParams(vmem_limit_bytes=VMEM_BYTES),
        cost_estimate=COST,
        name="source",
    )(*operands)


def spec_total(value):
    count = lax.axis_size("spec")
    if count & (count - 1):
        return lax.psum(value, "spec")
    reach = 1
    while reach < count:
        value = value + lax.ppermute(value, "spec", [(i, i ^ reach) for i in range(count)])
        reach *= 2
    return value


def relay_pairs(count, first_across):
    first, second = [], []
    for low in range(1, count - 1, 2):
        for source, goal in ((low + 1, low), (low, low + 1)):
            rank = low if source > goal else count - 2 - low
            if first_across(rank):
                middle = source ^ 1
            else:
                middle = goal if rank == 1 else goal ^ 1
            first.append((source, middle))
            second.append((middle, goal))
    return first, second


def along_pairs(count):
    first, second = [], []
    for low in range(1, count - 1, 2):
        for source, goal in ((low + 1, low), (low, low + 1)):
            first.append((source, goal ^ 1))
            second.append((goal ^ 1, goal))
    return first, second


def hold(value, *others):
    whole = pl.BlockSpec(memory_space=pl.ANY)
    return pl.pallas_call(
        lambda *refs: None,
        in_specs=[whole] * (1 + len(others)),
        out_specs=whole,
        out_shape=jax.ShapeDtypeStruct(value.shape, value.dtype),
        input_output_aliases={0: 0},
        cost_estimate=COST,
        name="hold",
    )(value, *others)


def shards(spectrum, land_sea, sea_index, sea_count, wind_speed, wind_dir, slope_x, slope_y):
    local_bands, dir_count, row_count, cols = spectrum.shape
    spec_count = lax.axis_size("spec")
    geo_count = lax.axis_size("geo")
    pos = lax.axis_index("spec").astype(jnp.int32)
    table = jnp.asarray(tables(local_bands * spec_count, dir_count))
    inner, outer, spill = (1, 2), (0, 3), 2
    kept = (1, 0, 3)
    size = min(2, local_bands)
    groups = list(range(0, local_bands, size))
    paired = local_bands == 4 and spec_count == 8
    meta = jnp.stack([pos, pos % 2 if paired else 0 * pos])
    choose = list(plan(land_sea, kept, spill, (0,), False))

    args = (meta, table, spectrum, land_sea, slope_x, slope_y)
    bands, sends, prior, rims, spills = {1: [], 2: []}, {}, [], [], []
    for group in groups[::-1]:
        strip_a, strip_b, send, sums, head, tail = propagate(
            inner, (0,), [((0,), 0, size, 0)], False, group, size, *args, prior, rims, [], choose[:1]
        )
        bands[1] = [(strip_a, i) for i in range(size)] + bands[1]
        bands[2] = [(strip_b, i) for i in range(size)] + bands[2]
        spills = [(strip_b, group, group + size)] + spills
        sends[1, group] = send
        prior, rims = [sums], [head, tail]
    ups = [(i, i + 1) for i in range(geo_count - 1)]
    downs = [(i + 1, i) for i in range(geo_count - 1)]
    rims = [lax.ppermute(tail, "geo", ups), lax.ppermute(head, "geo", downs)]
    choose += plan(land_sea, kept, spill, (1, 2), False)
    first, final = groups[0], groups[-1]
    if paired:
        outgoing = [((0,), 0, 1, SPARE), ((0,), 1, 1, SPARE), ((1,), 0, 2, 0), ((0, 1), 2, 2, 0)]
    else:
        outgoing = [((place,), group, size, 0) for group in sorted({first, final}) for place in (0, 1)]
    strip_a, strip_b, *outer_sends, sums = propagate(
        outer, (0, 1), outgoing, True, 0, local_bands, *args, prior, rims, spills, choose[1:]
    )
    bands[0] = [(strip_a, i) for i in range(local_bands)]
    bands[3] = [(strip_b, i) for i in range(local_bands)]
    scale = (28.0 * USTAR_RATIO / GRAVITY) * wind_speed
    wind = jnp.stack([scale * jnp.cos(wind_dir), scale * jnp.sin(wind_dir)])
    back = dict(zip(kept, plan(land_sea, kept, spill, (0, 1, 2), True)))

    def finish(s, halo, result, total, unpacked=False):
        if s != spill and not unpacked:
            total = unpack(halo, dir_count, back[s], total, land_sea if result is None else result)
        members = halo[:2] + bands[s] + halo[2:]
        result = source(s, spectrum.shape, meta, table, land_sea, wind, sums, s, members, result)
        return result, total

    result = total = None
    if paired:
        partner = [(i, i ^ 1) for i in range(spec_count)]
        across = relay_pairs(spec_count, lambda rank: True)
        most = relay_pairs(spec_count, lambda rank: 2 * rank >= spec_count - 2)
        some = relay_pairs(spec_count, lambda rank: rank >= spec_count - 3)
        along = along_pairs(spec_count)

        def send(value, pairs):
            return lax.ppermute(value, "spec", pairs)

        def members(far, near, slot):
            return [(far[-1], 2 - len(far)), (far[0], 0), (near, slot + 1), (near, slot)]

        near_1 = send(sends[1, final], partner)
        far_1 = send(sends[1, first], across[0])
        sums = sums + send(hold(sums, near_1), partner)
        near = send(hold(outer_sends[3], near_1), partner)
        others = [send(sums, [(i, i ^ k) for i in range(spec_count)]) for k in (2, 4, 6)]
        sums = (sums + others[0]) + (others[1] + others[2])
        far_3 = send(hold(outer_sends[2], sums), along[0])
        far_0 = [send(value, pairs[0]) for value, pairs in zip(outer_sends[:2], (some, most))]
        far_1 = send(far_1, across[1])
        far_3 = send(hold(far_3, far_1), along[1])
        halo = members([far_1], near_1, 0)
        total_far = unpack(halo[:2], dir_count, back[1], None, land_sea)
        total_near = unpack(halo[2:], dir_count, back[1], None, land_sea)
        result, _ = finish(1, halo, None, None, True)
        far_0 = [send(hold(value, result, total_far, total_near), pairs[1]) for value, pairs in zip(far_0, (some, most))]
        halo = {0: members(far_0, near, 0), 3: members([far_3], near, 2)}
        for s in (0, 3):
            total_near = unpack(halo[s][2:], dir_count, back[s], total_near, result)
        result, _ = finish(0, halo[0], result, None, True)
        parts = [halo[3][:2] + bands[3] + halo[3][2:]]
        parts.append([(None, 0), (None, 1)] + bands[spill] + [(total_near, 0), (total_near, 1)])
        unpacks, choosers = [halo[0][:2], halo[3][:2]], [back[0], back[3]]
        return last_sources(
            (3, spill), spectrum.shape, meta, table, land_sea, wind, sums, unpacks, parts, choosers, total_far, result
        )
    else:

        def hop(value, count):
            pairs = [(i, i + count) for i in range(spec_count) if 0 <= i + count < spec_count]
            return lax.ppermute(value, "spec", pairs)

        sums = spec_total(sums)
        places = [(group, place) for group in sorted({first, final}) for place in (0, 1)]
        for (group, place), array in zip(places, outer_sends):
            sends[kept[place + 1], group] = array
        for s in kept:
            low, high = sends[s, first], sends[s, final]
            if size == 2:
                lower, upper = hop(high, 1), hop(low, -1)
                halo = [(lower, 0), (lower, 1), (upper, 0), (upper, 1)]
            else:
                halo = [(hop(high, 2), 0), (hop(high, 1), 0), (hop(low, -1), 0), (hop(low, -2), 0)]
            result, total = finish(s, halo, result, total)
    return finish(spill, [(total, i) for i in range(4)], result, total)[0]


def solution(mesh):
    placed = (
        P("spec", None, "geo", None),
        P("geo", None),
        P("geo", None),
        P("geo"),
        P("geo", None),
        P("geo", None),
        P("geo", None),
        P("geo", None),
    )
    return jax.shard_map(
        shards, mesh=mesh, in_specs=placed, out_specs=P("spec", None, "geo", None), check_vma=False
    )
```

```python
import functools
import math

import jax
import jax.numpy as jnp
import numpy as np
from jax import lax
from jax.experimental import pallas as pl
from jax.experimental.pallas import tpu as pltpu
from jax.sharding import PartitionSpec as P

GRAVITY = 9.81
BASE_FREQ = 0.035
GROWTH = 1.1
COURANT_TOP = 0.9
TURN_TOP = 1.2
SPACING = 0.1
USTAR_RATIO = 0.035
WIND_COEF = 0.0375
WHITECAP = 0.36
STEEP_REF = 1.6
EPSILON = 1e-06
QUAD_COEF = 100.0

STRIP = 8
LANES = 128
VMEM_BYTES = 56 * 1024 * 1024
ROW_UNROLL = 9
TURN_UNROLL = 12
DELTA_UNROLL = 6
SOURCE_UNROLL = 6
SOURCE_LANES = 256
SPARE = 4
COST = pl.CostEstimate(flops=1024, bytes_accessed=1024, transcendentals=0)


def tables(band_total, dir_count):
    dtheta = 2.0 * math.pi / dir_count
    angles = (np.arange(dir_count) + 0.5) * dtheta
    faces = np.arange(dir_count) * dtheta
    parts = [
        np.abs(np.cos(angles)),
        np.abs(np.sin(angles)),
        np.sin(faces),
        np.cos(faces),
        np.cos(angles),
        np.sin(angles),
        GROWTH ** np.arange(band_total),
    ]
    return np.concatenate(parts).astype(np.float32)


def sign_runs(dir_count):
    angles = (np.arange(dir_count) + 0.5) * 2.0 * math.pi / dir_count
    signs = [(bool(np.cos(a) >= 0), bool(np.sin(a) >= 0)) for a in angles]
    runs, first = [], 0
    for j in range(1, dir_count + 1):
        if j == dir_count or signs[j] != signs[first]:
            runs.append((first, j) + signs[first])
            first = j
    return runs


def unrolled(first, last, count):
    def wrap(body):
        turns = (last - first) // count
        if turns:

            @pl.loop(0, turns)
            def _(turn):
                for k in range(count):
                    body(first + turn * count + k)

        for j in range(first + turns * count, last):
            body(j)

    return wrap


def plan_kernel(kept, spill, wanted, back, land_ref, *out_refs):
    cols = land_ref.shape[1]
    flags = [land_ref[STRIP * s : STRIP * s + 1, :].astype(jnp.float32) for s in (spill,) + tuple(kept)]
    rows = [flags[0]] + [1.0 - flag for flag in flags[1:]]
    rows += [jnp.zeros((1, cols), jnp.float32)] * (8 - len(rows))
    table = jnp.concatenate(rows, axis=0)
    first = lax.broadcasted_iota(jnp.int32, (cols, cols), 0)
    second = lax.broadcasted_iota(jnp.int32, (cols, cols), 1)
    block = STRIP
    starts = lax.broadcasted_iota(jnp.int32, (8, cols), 1) % block == 0
    narrow = jnp.where(starts, table, 0.0).astype(jnp.bfloat16)
    before = jnp.where(first < (second & ~(block - 1)), 1.0, 0.0).astype(jnp.bfloat16)
    ranks = jnp.dot(narrow, before, preferred_element_type=jnp.float32)
    phase = (first & (block - 1)) == (second & (block - 1))
    marks = [jnp.where(table[0:1] > 0.5, ranks[0:1], -1.0)]
    offset = jnp.zeros((1, 1), jnp.float32)
    for index in range(len(kept)):
        hole = table[index + 1 : index + 2, :]
        marks.append(jnp.where(hole > 0.5, ranks[index + 1 : index + 2, :] + offset, -2.0))
        offset = offset + jnp.sum(hole, axis=1, keepdims=True) * (1.0 / block)
    marks = jnp.concatenate(marks + [jnp.zeros((1, cols), jnp.float32)] * (8 - len(marks)), axis=0)
    columns = marks.T
    for index, out_ref in zip(wanted, out_refs):
        if back:
            match = jnp.abs(columns[:, index + 1 : index + 2] - marks[0:1, :]) < 0.5
        else:
            match = jnp.abs(columns[:, 0:1] - marks[index + 1 : index + 2, :]) < 0.5
        out_ref[...] = jnp.where(jnp.logical_and(phase, match), 1.0, 0.0).astype(jnp.bfloat16)


def plan(land_sea, kept, spill, wanted, back):
    cols = land_sea.shape[1]
    return pl.pallas_call(
        functools.partial(plan_kernel, kept, spill, wanted, back),
        out_shape=[jax.ShapeDtypeStruct((cols, cols), jnp.bfloat16)] * len(wanted),
        compiler_params=pltpu.CompilerParams(vmem_limit_bytes=VMEM_BYTES),
        name="plan_back" if back else "plan",
    )(land_sea)


def taps(courant):
    rest = (1.0 - courant * courant) * (1.0 / 6.0)
    down = courant * (0.5 - 0.5 * courant - rest)
    centre = courant * (0.5 + 0.5 * courant + 2.0 * rest)
    far = -courant * rest
    return -down, 1.0 - centre + down, centre - far, far


def lane_shift(pieces, shift, lane_ids):
    rolled = [pltpu.roll(piece, shift % LANES, 1) for piece in pieces]
    zero = jnp.zeros_like(pieces[0])
    moved = []
    for index in range(len(pieces)):
        if shift > 0:
            other = rolled[index - 1] if index > 0 else zero
            moved.append(jnp.where(lane_ids < shift, other, rolled[index]))
        else:
            other = rolled[index + 1] if index + 1 < len(pieces) else zero
            moved.append(jnp.where(lane_ids >= LANES + shift, other, rolled[index]))
    return moved


def split_store(cells, split_ref):
    count = cells.shape[0]
    high = cells.astype(jnp.bfloat16)
    rest = cells - high.astype(jnp.float32)
    mid = rest.astype(jnp.bfloat16)
    split_ref[0:count, :] = high
    split_ref[count : 2 * count, :] = mid


def local_band(index, flip, local_bands):
    return index + flip * (local_bands - 1 - 2 * index)


def take(refs, count):
    return refs[:count], refs[count:]


def propagate_kernel(strips, dests, sends, spills, edge, chained, rims, group, size, dir_count, local_bands, *refs):
    (meta_ref, tab_ref, spec_ref, land_ref, sx_ref, sy_ref), refs = take(list(refs), 6)
    prior_refs, refs = take(refs, chained)
    rim_refs, refs = take(refs, 2 if edge or rims else 0)
    spill_refs, refs = take(refs, len(spills))
    choosers, refs = take(refs, len(dests))
    out_refs, refs = take(refs, len(strips))
    send_refs, refs = take(refs, len(sends))
    (sum_ref,), refs = take(refs, 1)
    edge_refs, refs = take(refs, 0 if edge else 2)
    turn_ref, moved_ref, split_ref, wet_ref = refs

    row_count, cols = land_ref.shape
    strip_count = row_count // STRIP
    step = pl.program_id(0)
    band = meta_ref[0] * local_bands + local_band(group + step, meta_ref[1], local_bands)
    growth = tab_ref[6 * dir_count + band]
    courant = COURANT_TOP / growth
    turn_rate = TURN_TOP / growth
    radian_freq = (2.0 * math.pi * BASE_FREQ) * growth
    weight = SPACING * radian_freq * (2.0 * math.pi / dir_count)
    row_ids = lax.broadcasted_iota(jnp.int32, (STRIP, cols), 0)
    lane_ids = lax.broadcasted_iota(jnp.int32, (STRIP, LANES), 1)

    @pl.when(step == 0)
    def _():
        sum_ref[...] = prior_refs[0][...] if chained else jnp.zeros_like(sum_ref)
        wet_ref[...] = land_ref[...].astype(jnp.float32)
        if rims:
            for edge_ref, rim_ref in zip(edge_refs, rim_refs):
                edge_ref[...] = rim_ref[...]

        @pl.loop(0, dir_count)
        def _(f):
            face_sin = tab_ref[2 * dir_count + f]
            face_cos = tab_ref[3 * dir_count + f]
            for slot, s in enumerate(strips):
                rows = slice(STRIP * s, STRIP * (s + 1))
                turn_ref[slot, f] = face_sin * sx_ref[rows, :] - face_cos * sy_ref[rows, :]

    for first, last, cos_up, sin_up in sign_runs(dir_count):

        @unrolled(first, last, ROW_UNROLL)
        def _(j):
            row_taps = taps(courant * tab_ref[j])
            col_taps = taps(courant * tab_ref[dir_count + j])
            known = {}

            def wet(s):
                return wet_ref[STRIP * s : STRIP * (s + 1), :]

            def cells(s):
                if s not in known:
                    if s < 0:
                        blank = jnp.zeros((STRIP - 2, cols), jnp.float32)
                        known[s] = jnp.concatenate([blank, rim_refs[0][0, j]], axis=0)
                    elif s == strip_count:
                        blank = jnp.zeros((STRIP - 2, cols), jnp.float32)
                        known[s] = jnp.concatenate([rim_refs[1][0, j], blank], axis=0)
                    else:
                        known[s] = spec_ref[0, j, STRIP * s : STRIP * (s + 1), :] * wet(s)
                return known[s]

            def rolled(s, shift):
                if (s, shift) not in known:
                    known[s, shift] = pltpu.roll(cells(s), shift % STRIP, 0)
                return known[s, shift]

            def row_shift(s, shift):
                other = rolled(s - 1 if shift > 0 else s + 1, shift)
                outside = row_ids < shift if shift > 0 else row_ids >= STRIP + shift
                return jnp.where(outside, other, rolled(s, shift))

            if not edge:
                edge_refs[0][group + step, j] = cells(0)[0:2]
                edge_refs[1][group + step, j] = cells(strip_count - 1)[STRIP - 2 :]
            for slot, s in enumerate(strips):
                wet_s = wet(s)
                way = 1 if cos_up else -1
                moved = (
                    row_taps[1] * cells(s)
                    + row_taps[0] * row_shift(s, -way)
                    + row_taps[2] * row_shift(s, way)
                    + row_taps[3] * row_shift(s, 2 * way)
                ) * wet_s
                way = 1 if sin_up else -1
                pieces = [moved[:, LANES * c : LANES * (c + 1)] for c in range(cols // LANES)]
                down = lane_shift(pieces, -way, lane_ids)
                upwind = lane_shift(pieces, way, lane_ids)
                far = lane_shift(pieces, 2 * way, lane_ids)
                for c in range(cols // LANES):
                    lanes = slice(LANES * c, LANES * (c + 1))
                    moved_ref[slot, j + 2, :, lanes] = (
                        col_taps[1] * pieces[c]
                        + col_taps[0] * down[c]
                        + col_taps[2] * upwind[c]
                        + col_taps[3] * far[c]
                    ) * wet_s[:, lanes]

    moved_ref[:, 0:2] = moved_ref[:, dir_count : dir_count + 2]
    moved_ref[:, dir_count + 2 : dir_count + 4] = moved_ref[:, 2:4]

    def face_flux(slot, f, turning):
        far_left, left = moved_ref[slot, f], moved_ref[slot, f + 1]
        right, far_right = moved_ref[slot, f + 2], moved_ref[slot, f + 3]
        rate = turn_rate * turning
        square = rate * rate
        slope = right - left
        bend = jnp.where(rate >= 0, slope - (left - far_left), (far_right - right) - slope)
        return rate * (
            0.5 * ((left + right) - rate * slope) - (1.0 / 6.0 - square * (1.0 / 6.0)) * bend
        )

    def turn(step, carry):
        carry = list(carry)
        for k in range(TURN_UNROLL):
            f = step * TURN_UNROLL + k + 1
            face = f if k < TURN_UNROLL - 1 else lax.rem(f, dir_count)
            for slot in range(len(strips)):
                lower, total = carry[slot]
                flux = face_flux(slot, f, turn_ref[slot, face])
                cell = jnp.maximum(moved_ref[slot, f + 1] - (flux - lower), 0.0)
                out_refs[slot][0, f - 1] = cell
                carry[slot] = (flux, total + cell)
        return tuple(carry)

    zero = jnp.zeros((STRIP, cols), jnp.float32)
    start = tuple((face_flux(slot, 0, turn_ref[slot, 0]), zero) for slot in range(len(strips)))
    ends = lax.fori_loop(0, dir_count // TURN_UNROLL, turn, start)
    for slot, (_, total) in enumerate(ends):
        rows = slice(STRIP * strips[slot], STRIP * (strips[slot] + 1))
        sum_ref[0, rows, :] += weight * total
        sum_ref[1, rows, :] += (SPACING * 2.0 * math.pi / dir_count) * total

    count = dir_count * STRIP
    if spills:
        for (low, high), spill_ref in zip(spills, spill_refs):

            @pl.when(jnp.logical_and(step >= low, step < high))
            def _():
                split_store(spill_ref[0].reshape(count, cols), split_ref)

    else:
        split_store(out_refs[-1][0].reshape(count, cols), split_ref)
    filled = []
    for chooser, dest in zip(choosers, dests):
        product = jnp.dot(split_ref[...], chooser[...], preferred_element_type=jnp.float32)
        product = product[0:count] + product[count : 2 * count]
        filled.append(out_refs[dest][0] + product.reshape(dir_count, STRIP, cols))
    for (places, low, length, _), send_ref in zip(sends, send_refs):

        @pl.when(jnp.logical_and(step >= low, step < low + length))
        def _():
            for index, place in enumerate(places):
                start = (index * length + step - low) * dir_count
                send_ref[pl.ds(start, dir_count)] = filled[place]


def propagate(strips, dests, sends, edge, group, size, meta, table, spectrum, land_sea, slope_x, slope_y, prior, rims, spills, choosers):
    local_bands, dir_count, row_count, cols = spectrum.shape
    whole = lambda shape: pl.BlockSpec(shape, lambda b, meta: (0,) * len(shape))
    clip = lambda b, low, length: jnp.clip(b - low, 0, length - 1)
    flat = whole((row_count, cols))
    in_specs = [pl.BlockSpec(memory_space=pltpu.SMEM)]
    in_specs += [
        pl.BlockSpec(
            (1, dir_count, row_count, cols),
            lambda b, meta: (local_band(b + group, meta[1], local_bands), 0, 0, 0),
        )
    ]
    in_specs += [flat, flat, flat]
    sums = (2, row_count, cols)
    in_specs += [whole(sums)] * len(prior)
    if edge:
        in_specs += [pl.BlockSpec((1, dir_count, 2, cols), lambda b, meta: (b, 0, 0, 0))] * 2
    else:
        in_specs += [whole(rim.shape) for rim in rims]
    for _, low, high in spills:
        in_specs.append(
            pl.BlockSpec(
                (1, dir_count, STRIP, cols), lambda b, meta, low=low, high=high: (clip(b, low, high - low), 0, 0, 0)
            )
        )
    in_specs += [whole((cols, cols))] * len(choosers)
    shape = lambda *dims: jax.ShapeDtypeStruct(dims, jnp.float32)
    out_shape = [shape(size, dir_count, STRIP, cols)] * len(strips)
    out_specs = [pl.BlockSpec((1, dir_count, STRIP, cols), lambda b, meta: (b, 0, 0, 0))] * len(strips)
    for places, low, length, room in sends:
        block = (len(places) * length * dir_count + room, STRIP, cols)
        out_shape.append(shape(*block))
        out_specs.append(whole(block))
    out_shape.append(shape(*sums))
    out_specs.append(whole(sums))
    if not edge:
        out_shape += [shape(local_bands, dir_count, 2, cols)] * 2
        out_specs += [whole((local_bands, dir_count, 2, cols))] * 2
    return pl.pallas_call(
        functools.partial(
            propagate_kernel,
            strips,
            dests,
            sends,
            [(low, high) for _, low, high in spills],
            edge,
            len(prior),
            not edge and len(rims) > 0,
            group,
            size,
            dir_count,
            local_bands,
        ),
        grid_spec=pltpu.PrefetchScalarGridSpec(
            num_scalar_prefetch=1,
            grid=(size,),
            in_specs=in_specs,
            out_specs=out_specs,
            scratch_shapes=[
                pltpu.VMEM((len(strips), dir_count, STRIP, cols), jnp.float32),
                pltpu.VMEM((len(strips), dir_count + 4, STRIP, cols), jnp.float32),
                pltpu.VMEM((2 * dir_count * STRIP, cols), jnp.bfloat16),
                pltpu.VMEM((row_count, cols), jnp.float32),
            ],
        ),
        out_shape=out_shape,
        compiler_params=pltpu.CompilerParams(vmem_limit_bytes=VMEM_BYTES),
        cost_estimate=COST,
        name="propagate_edge" if edge else "propagate_inner",
    )(meta, table, spectrum, land_sea, slope_x, slope_y, *prior, *rims, *[spill[0] for spill in spills], *choosers)


def unpack_kernel(places, has_total, *refs):
    out_ref, split_ref = refs[-2:]
    total_ref, chooser_ref = refs[-4], refs[-4 - has_total]
    _, dir_count, rows, cols = out_ref.shape
    count = dir_count * rows
    for slot, place in enumerate(places):

        @pl.when(pl.program_id(0) == slot)
        def _():
            split_store(refs[place][...].reshape(count, cols), split_ref)

    product = jnp.dot(split_ref[...], chooser_ref[...], preferred_element_type=jnp.float32)
    cells = product[0:count] + product[count : 2 * count]
    cells = cells.reshape(dir_count, rows, cols)
    out_ref[0] = cells + total_ref[0] if has_total else cells


def slot_map(uses, slots):
    held = []
    for use, slot in zip(uses, slots):
        held.append(slot if use else (held[-1] if held else None))
    first = next(slot for slot in held if slot is not None)
    held = [first if slot is None else slot for slot in held]

    def index(step):
        place = held[0]
        for k in range(1, len(held)):
            place = place + jnp.where(step >= k, held[k] - held[k - 1], 0)
        return place

    return index


def flat_bands(array):
    return array.reshape((-1,) + array.shape[-2:])


def unpack(halo, dir_count, chooser, total, after):
    arrays = distinct(halo)
    places = [next(i for i, a in enumerate(arrays) if a is array) for array, _ in halo]
    rows, cols = arrays[0].shape[-2:]
    block = (1, dir_count, rows, cols)
    in_specs = []
    for i in range(len(arrays)):
        index = slot_map([place == i for place in places], [slot for _, slot in halo])
        in_specs.append(pl.BlockSpec(block[1:], lambda b, index=index: (index(b), 0, 0)))
    one = pl.BlockSpec(block, lambda b: (b, 0, 0, 0))
    in_specs.append(pl.BlockSpec(chooser.shape, lambda b: (0, 0)))
    extra = [] if total is None else [total]
    in_specs += [one] * len(extra)
    in_specs.append(pl.BlockSpec(memory_space=pl.ANY))
    return pl.pallas_call(
        functools.partial(unpack_kernel, places, len(extra)),
        grid=(len(halo),),
        in_specs=in_specs,
        out_specs=one,
        out_shape=jax.ShapeDtypeStruct((len(halo),) + block[1:], jnp.float32),
        scratch_shapes=[pltpu.VMEM((2 * dir_count * rows, cols), jnp.bfloat16)],
        compiler_params=pltpu.CompilerParams(vmem_limit_bytes=VMEM_BYTES),
        cost_estimate=COST,
        name="unpack",
    )(*[flat_bands(array) for array in arrays], chooser, *extra, after)


def distinct(halo):
    arrays = []
    for array, _ in halo:
        if not any(array is other for other in arrays):
            arrays.append(array)
    return arrays


def source_kernel(dir_count, local_bands, places, *refs):
    bands = [(refs[5 + place], slot) for place, slot in places]

    def density(index, j):
        ref, slot = bands[index + 2]
        return ref[slot * dir_count + j]

    source_body(dir_count, local_bands, density, *refs[:5], *refs[-2:])


def source_body(dir_count, local_bands, density, meta_ref, tab_ref, land_ref, wind_ref, sum_ref, out_ref, delta_ref):
    flip = meta_ref[1]
    energy = sum_ref[0] + EPSILON
    first_sum = sum_ref[1]
    mean_sigma = energy / (first_sum + EPSILON)
    ratio = energy / (math.sqrt(GRAVITY) * first_sum + EPSILON)
    mean_k = ratio * ratio
    steepness = energy * mean_k * mean_k / STEEP_REF
    decay = WHITECAP * mean_sigma / mean_k * steepness * steepness
    active = land_ref[...].astype(jnp.float32)
    quad_scale = active * QUAD_COEF / (energy * energy)

    @unrolled(0, dir_count, DELTA_UNROLL)
    def _(j):
        up = lax.rem(j + dir_count + 1 - 4 * flip, dir_count)
        back = lax.rem(j + dir_count - 3 + 4 * flip, dir_count)
        for index in range(-1, local_bands + 1):
            center = density(index, j)
            plus = density(index + 1, up)
            minus = density(index - 1, back)
            delta_ref[index + 1, j] = center * (center * (plus + minus) - 2.0 * (plus * minus))

    growths, keeps, homes = [], [], []
    for index in range(local_bands):
        homes.append(local_band(index, flip, local_bands))
        growth = tab_ref[6 * dir_count + meta_ref[0] * local_bands + homes[index]]
        radian_freq = (2.0 * math.pi * BASE_FREQ) * growth
        wavenum = radian_freq * radian_freq * (1.0 / GRAVITY)
        growths.append(radian_freq)
        keeps.append(active / (1.0 + decay * wavenum))

    @unrolled(0, dir_count, SOURCE_UNROLL)
    def _(j):
        up = lax.rem(j + dir_count + 3 - 4 * flip, dir_count)
        back = lax.rem(j + dir_count - 1 + 4 * flip, dir_count)
        wind = tab_ref[4 * dir_count + j] * wind_ref[0] + tab_ref[5 * dir_count + j] * wind_ref[1]
        for index in range(local_bands):
            radian_freq = growths[index]
            quad = delta_ref[index, back] + delta_ref[index + 2, up] - 2.0 * delta_ref[index + 1, j]
            rate = WIND_COEF * radian_freq
            gain = jnp.maximum((rate * radian_freq) * wind + (1.0 - rate), 1.0)
            out_ref[homes[index], j] = density(index, j) * gain * keeps[index] + quad * quad_scale


def spans_of(bands):
    arrays = distinct(bands)
    spans = []
    for array in arrays:
        slots = [slot for other, slot in bands if other is array]
        low, count = min(slots), max(slots) - min(slots) + 1
        spans.append((low // count, count) if low % count == 0 else (0, max(slots) + 1))
    places = []
    for array, slot in bands:
        index = next(i for i, a in enumerate(arrays) if a is array)
        places.append((index, slot - spans[index][0] * spans[index][1]))
    return arrays, spans, places


def last_kernel(dir_count, local_bands, halves, unpack_places, band_places, counts, *refs):
    scalar, refs = take(list(refs), 5)
    halo_refs = []
    for count in counts[0]:
        found, refs = take(refs, count)
        halo_refs.append(found)
    (prior_ref, *choosers), refs = take(refs, 1 + len(unpack_places))
    band_refs = []
    for count in counts[1]:
        found, refs = take(refs, count)
        band_refs.append(found)
    _, out_ref, delta_ref, split_ref, total_ref = refs
    step = pl.program_id(0)
    halo_count = len(unpack_places[0])
    _, rows, cols = halo_refs[0][0].shape
    lanes = out_ref.shape[-1]
    count = dir_count * rows

    @pl.when(step < halo_count)
    def _():
        total = prior_ref[...]
        for found, places, chooser in zip(halo_refs, unpack_places, choosers):
            for slot, place in enumerate(places):

                @pl.when(step == slot)
                def _():
                    split_store(found[place][...].reshape(count, cols), split_ref)

            product = jnp.dot(split_ref[...], chooser[...], preferred_element_type=jnp.float32)
            total = total + (product[0:count] + product[count : 2 * count]).reshape(dir_count, rows, cols)
        for half in range(halves):
            total_ref[half, pl.ds(step * dir_count, dir_count)] = total[:, :, half * lanes : (half + 1) * lanes]

    half = lax.rem(jnp.maximum(step - halo_count, 0), halves)
    for turn, (found, places) in enumerate(zip(band_refs, band_places)):
        first = halo_count + turn * halves

        @pl.when(jnp.logical_and(step >= first, step < first + halves))
        def _():
            def density(index, j):
                place, slot = places[index + 2]
                if place is None:
                    return total_ref[half, slot * dir_count + j]
                return found[place][slot * dir_count + j]

            source_body(dir_count, local_bands, density, *scalar, out_ref, delta_ref)


def last_sources(strips, shape, meta, table, land_sea, wind, sums, halos, members, choosers, total, previous):
    local_bands, dir_count, row_count, cols = shape
    lanes = SOURCE_LANES if cols % SOURCE_LANES == 0 else cols
    halves = cols // lanes
    halo_count = len(halos[0])
    smem = pl.BlockSpec(memory_space=pltpu.SMEM)

    def turn(t):
        return jnp.maximum(t - halo_count, 0) // halves

    def strip(t):
        place = strips[0]
        for k in range(1, len(strips)):
            place = place + jnp.where(turn(t) >= k, strips[k] - strips[k - 1], 0)
        return place

    def half(t):
        return lax.rem(jnp.maximum(t - halo_count, 0), halves)

    def part(t, k):
        return jnp.clip(t - halo_count - k * halves, 0, halves - 1)

    in_specs = [smem, smem]
    in_specs.append(pl.BlockSpec((STRIP, lanes), lambda t: (strip(t), half(t))))
    in_specs += [pl.BlockSpec((2, STRIP, lanes), lambda t: (0, strip(t), half(t)))] * 2
    operands = [meta, table, land_sea, wind, sums]
    block = (dir_count, STRIP, cols)
    unpack_places, counts = [], ([], [])
    for halo in halos:
        arrays = distinct(halo)
        places = [next(i for i, a in enumerate(arrays) if a is array) for array, _ in halo]
        for i, array in enumerate(arrays):
            index = slot_map([place == i for place in places], [slot for _, slot in halo])
            in_specs.append(pl.BlockSpec(block, lambda t, index=index: (index(t), 0, 0)))
            operands.append(flat_bands(array))
        unpack_places.append(places)
        counts[0].append(len(arrays))
    in_specs.append(pl.BlockSpec(block, lambda t: (jnp.minimum(t, halo_count - 1), 0, 0)))
    operands.append(flat_bands(total))
    in_specs += [pl.BlockSpec((cols, cols), lambda t: (0, 0))] * len(choosers)
    operands += choosers
    band_places = []
    for k in range(len(strips)):
        arrays, spans, found = spans_of([entry for entry in members[k] if entry[0] is not None])
        found = iter(found)
        places = [(None, slot) if array is None else next(found) for array, slot in members[k]]
        for array, (first, count) in zip(arrays, spans):
            in_specs.append(
                pl.BlockSpec(
                    (count * dir_count, STRIP, lanes), lambda t, first=first, k=k: (first, 0, part(t, k))
                )
            )
            operands.append(flat_bands(array))
        band_places.append(places)
        counts[1].append(len(arrays))
    in_specs.append(pl.BlockSpec(memory_space=pl.ANY))
    operands.append(previous)
    return pl.pallas_call(
        functools.partial(last_kernel, dir_count, local_bands, halves, unpack_places, band_places, counts),
        grid=(halo_count + len(strips) * halves,),
        in_specs=in_specs,
        out_specs=pl.BlockSpec((local_bands, dir_count, STRIP, lanes), lambda t: (0, 0, strip(t), half(t))),
        out_shape=jax.ShapeDtypeStruct(shape, jnp.float32),
        scratch_shapes=[
            pltpu.VMEM((local_bands + 2, dir_count, STRIP, lanes), jnp.float32),
            pltpu.VMEM((2 * dir_count * STRIP, cols), jnp.bfloat16),
            pltpu.VMEM((halves, halo_count * dir_count, STRIP, lanes), jnp.float32),
        ],
        input_output_aliases={len(operands) - 1: 0},
        compiler_params=pltpu.CompilerParams(vmem_limit_bytes=VMEM_BYTES),
        cost_estimate=COST,
        name="last_sources",
    )(*operands)


def source(strip, shape, meta, table, land_sea, wind, sums, sum_block, bands, previous):
    local_bands, dir_count, row_count, cols = shape
    lanes = SOURCE_LANES if cols % SOURCE_LANES == 0 else cols
    arrays, spans, places = spans_of(bands)
    smem = pl.BlockSpec(memory_space=pltpu.SMEM)
    part = lambda first, count: pl.BlockSpec((count * dir_count, STRIP, lanes), lambda c: (first, 0, c))
    in_specs = [smem, smem]
    in_specs.append(pl.BlockSpec((STRIP, lanes), lambda c: (strip, c)))
    in_specs.append(pl.BlockSpec((2, STRIP, lanes), lambda c: (0, strip, c)))
    in_specs.append(pl.BlockSpec((2, STRIP, lanes), lambda c: (0, sum_block, c)))
    in_specs += [part(*span) for span in spans]
    operands = [meta, table, land_sea, wind, sums, *[flat_bands(array) for array in arrays]]
    aliases = {}
    if previous is not None:
        in_specs.append(pl.BlockSpec(memory_space=pl.ANY))
        aliases = {len(operands): 0}
        operands.append(previous)
    return pl.pallas_call(
        functools.partial(source_kernel, dir_count, local_bands, places),
        grid=(cols // lanes,),
        in_specs=in_specs,
        out_specs=pl.BlockSpec((local_bands, dir_count, STRIP, lanes), lambda c: (0, 0, strip, c)),
        out_shape=jax.ShapeDtypeStruct(shape, jnp.float32),
        scratch_shapes=[pltpu.VMEM((local_bands + 2, dir_count, STRIP, lanes), jnp.float32)],
        input_output_aliases=aliases,
        compiler_params=pltpu.CompilerParams(vmem_limit_bytes=VMEM_BYTES),
        cost_estimate=COST,
        name="source",
    )(*operands)


def spec_total(value):
    count = lax.axis_size("spec")
    if count & (count - 1):
        return lax.psum(value, "spec")
    reach = 1
    while reach < count:
        value = value + lax.ppermute(value, "spec", [(i, i ^ reach) for i in range(count)])
        reach *= 2
    return value


def relay_pairs(count, first_across):
    first, second = [], []
    for low in range(1, count - 1, 2):
        for source, goal in ((low + 1, low), (low, low + 1)):
            rank = low if source > goal else count - 2 - low
            if first_across(rank):
                middle = source ^ 1
            else:
                middle = goal if rank == 1 else goal ^ 1
            first.append((source, middle))
            second.append((middle, goal))
    return first, second


def by_tile(count, tiles, even, odd):
    steps = ([], [])
    for tile in range(tiles):
        for step, pairs in zip(steps, odd if tile % 2 else even):
            step.extend((tile * count + source, tile * count + goal) for source, goal in pairs)
    return steps


def along_pairs(count):
    first, second = [], []
    for low in range(1, count - 1, 2):
        for source, goal in ((low + 1, low), (low, low + 1)):
            first.append((source, goal ^ 1))
            second.append((goal ^ 1, goal))
    return first, second


def hold(value, *others):
    whole = pl.BlockSpec(memory_space=pl.ANY)
    return pl.pallas_call(
        lambda *refs: None,
        in_specs=[whole] * (1 + len(others)),
        out_specs=whole,
        out_shape=jax.ShapeDtypeStruct(value.shape, value.dtype),
        input_output_aliases={0: 0},
        cost_estimate=COST,
        name="hold",
    )(value, *others)


def shards(spectrum, land_sea, sea_index, sea_count, wind_speed, wind_dir, slope_x, slope_y):
    local_bands, dir_count, row_count, cols = spectrum.shape
    spec_count = lax.axis_size("spec")
    geo_count = lax.axis_size("geo")
    pos = lax.axis_index("spec").astype(jnp.int32)
    table = jnp.asarray(tables(local_bands * spec_count, dir_count))
    inner, outer, spill = (1, 2), (0, 3), 2
    kept = (1, 0, 3)
    size = min(2, local_bands)
    groups = list(range(0, local_bands, size))
    paired = local_bands == 4 and spec_count == 8
    meta = jnp.stack([pos, pos % 2 if paired else 0 * pos])
    choose = list(plan(land_sea, kept, spill, (0,), False))

    args = (meta, table, spectrum, land_sea, slope_x, slope_y)
    bands, sends, prior, rims, spills = {1: [], 2: []}, {}, [], [], []
    for group in groups[::-1]:
        strip_a, strip_b, send, sums, head, tail = propagate(
            inner, (0,), [((0,), 0, size, 0)], False, group, size, *args, prior, rims, [], choose[:1]
        )
        bands[1] = [(strip_a, i) for i in range(size)] + bands[1]
        bands[2] = [(strip_b, i) for i in range(size)] + bands[2]
        spills = [(strip_b, group, group + size)] + spills
        sends[1, group] = send
        prior, rims = [sums], [head, tail]
    ups = [(i, i + 1) for i in range(geo_count - 1)]
    downs = [(i + 1, i) for i in range(geo_count - 1)]
    rims = [lax.ppermute(tail, "geo", ups), lax.ppermute(head, "geo", downs)]
    choose += plan(land_sea, kept, spill, (1, 2), False)
    first, final = groups[0], groups[-1]
    if paired:
        outgoing = [((0,), 0, 1, SPARE), ((0,), 1, 1, SPARE), ((1,), 0, 2, 0), ((0, 1), 2, 2, 0)]
    else:
        outgoing = [((place,), group, size, 0) for group in sorted({first, final}) for place in (0, 1)]
    strip_a, strip_b, *outer_sends, sums = propagate(
        outer, (0, 1), outgoing, True, 0, local_bands, *args, prior, rims, spills, choose[1:]
    )
    bands[0] = [(strip_a, i) for i in range(local_bands)]
    bands[3] = [(strip_b, i) for i in range(local_bands)]
    scale = (28.0 * USTAR_RATIO / GRAVITY) * wind_speed
    wind = jnp.stack([scale * jnp.cos(wind_dir), scale * jnp.sin(wind_dir)])
    back = dict(zip(kept, plan(land_sea, kept, spill, (0, 1, 2), True)))

    def finish(s, halo, result, total, unpacked=False):
        if s != spill and not unpacked:
            total = unpack(halo, dir_count, back[s], total, land_sea if result is None else result)
        members = halo[:2] + bands[s] + halo[2:]
        result = source(s, spectrum.shape, meta, table, land_sea, wind, sums, s, members, result)
        return result, total

    result = total = None
    if paired:
        partner = [(i, i ^ 1) for i in range(spec_count)]
        across = relay_pairs(spec_count, lambda rank: True)
        most = relay_pairs(spec_count, lambda rank: 2 * rank >= spec_count - 2)
        some = relay_pairs(spec_count, lambda rank: rank >= spec_count - 3)
        along = along_pairs(spec_count)

        def send(value, pairs):
            return lax.ppermute(value, "spec", pairs)

        def members(far, near, slot):
            return [(far[-1], 2 - len(far)), (far[0], 0), (near, slot + 1), (near, slot)]

        near_1 = send(sends[1, final], partner)
        far_1 = send(sends[1, first], across[0])
        sums = sums + send(hold(sums, near_1), partner)
        near = send(hold(outer_sends[3], near_1), partner)
        others = [send(sums, [(i, i ^ k) for i in range(spec_count)]) for k in (2, 4, 6)]
        sums = (sums + others[0]) + (others[1] + others[2])
        far_3 = send(hold(outer_sends[2], sums), along[0])
        mixed = by_tile(spec_count, geo_count, some, relay_pairs(spec_count, lambda rank: rank != 3))
        far_0 = [lax.ppermute(outer_sends[0], ("geo", "spec"), mixed[0]), send(outer_sends[1], most[0])]
        far_1 = send(far_1, across[1])
        far_3 = send(hold(far_3, far_1), along[1])
        halo = members([far_1], near_1, 0)
        total_far = unpack(halo[:2], dir_count, back[1], None, land_sea)
        total_near = unpack(halo[2:], dir_count, back[1], None, land_sea)
        result, _ = finish(1, halo, None, None, True)
        far_0 = [hold(value, result, total_far, total_near) for value in far_0]
        far_0 = [lax.ppermute(far_0[0], ("geo", "spec"), mixed[1]), send(far_0[1], most[1])]
        halo = {0: members(far_0, near, 0), 3: members([far_3], near, 2)}
        for s in (0, 3):
            total_near = unpack(halo[s][2:], dir_count, back[s], total_near, result)
        result, _ = finish(0, halo[0], result, None, True)
        parts = [halo[3][:2] + bands[3] + halo[3][2:]]
        parts.append([(None, 0), (None, 1)] + bands[spill] + [(total_near, 0), (total_near, 1)])
        unpacks, choosers = [halo[0][:2], halo[3][:2]], [back[0], back[3]]
        return last_sources(
            (3, spill), spectrum.shape, meta, table, land_sea, wind, sums, unpacks, parts, choosers, total_far, result
        )
    else:

        def hop(value, count):
            pairs = [(i, i + count) for i in range(spec_count) if 0 <= i + count < spec_count]
            return lax.ppermute(value, "spec", pairs)

        sums = spec_total(sums)
        places = [(group, place) for group in sorted({first, final}) for place in (0, 1)]
        for (group, place), array in zip(places, outer_sends):
            sends[kept[place + 1], group] = array
        for s in kept:
            low, high = sends[s, first], sends[s, final]
            if size == 2:
                lower, upper = hop(high, 1), hop(low, -1)
                halo = [(lower, 0), (lower, 1), (upper, 0), (upper, 1)]
            else:
                halo = [(hop(high, 2), 0), (hop(high, 1), 0), (hop(low, -1), 0), (hop(low, -2), 0)]
            result, total = finish(s, halo, result, total)
    return finish(spill, [(total, i) for i in range(4)], result, total)[0]


def solution(mesh):
    placed = (
        P("spec", None, "geo", None),
        P("geo", None),
        P("geo", None),
        P("geo"),
        P("geo", None),
        P("geo", None),
        P("geo", None),
        P("geo", None),
    )
    return jax.shard_map(
        shards, mesh=mesh, in_specs=placed, out_specs=P("spec", None, "geo", None), check_vma=False
    )
```
